256 devices in a mesh: section: 16 (over x_hi, z), dp: 16 (over x_lo, y, core).
Axes of the slice: x: 4 (x_hi: 2, x_lo: 2; x = x_hi * 2 + x_lo), y: 4, z: 8, core: 2. Of those that a mesh axis runs over, the one named last changes fastest.
Arguments:
- saved_inputs: bfloat16 [16, 32, 256, 2560], P('section', 'dp'), may hold values from -20 to 20
- query_gains: float32 [16, 2560], P('section'), may hold values from 0.5 to 1.5
- cache_slots: bfloat16 [16, 32, 256, 1024], P('section', 'dp'), may hold values from -4 to 4
- segment_ids: int32 [32, 256], P('dp'), may hold values from 0 to 4, as said below
- output_grad: bfloat16 [32, 256, 2560], P('dp'), may hold values from -6 to 6
Outputs:
- layer_grads: bfloat16 [16, 32, 256, 2560], P('section', 'dp')
- cache_grad: bfloat16 [32, 256, 1024], P('dp')
- gain_grads: float32 [16, 2560], P('section')
The draws below stay inside these ranges and needn't reach their ends.
Inputs may be any that keep to these rules, and one draw needn't show every extreme that they name: `segment_ids`: along each row the ids start at 0, never fall, rise by at most one and end at 4; every segment begins at an even position.
All inputs are finite; a program needn't handle non-finite values.
Results may differ from the reference program's by a relative error of at most 0.0092.
Values may be sent and summed in bfloat16 or wider, within the bound.
No kernel may reach another device: no remote copies, remote signals or barrier semaphores. Data moves between devices by JAX's collectives and lax.ppermute only.
A program may use at most 128 MiB of HBM per device.

```python
import jax
import jax.numpy as jnp
from jax import lax

HEADS = 20
KV_HEADS = 4
HEAD = 128
SEQ = 256
BATCH = 32
N_SECTION = 16


def shared_keys(key):
    return jnp.clip(jax.random.normal(key, (BATCH, SEQ, KV_HEADS * HEAD), jnp.float32), -4.0, 4.0)


def draw_saved_inputs(key, part):
    key = jax.random.fold_in(key, 7)
    first_key = jax.random.fold_in(key, 0)
    shape = (N_SECTION, BATCH, SEQ, HEADS * HEAD)
    base = jnp.clip(jax.random.normal(first_key, shape, jnp.float32), -4.0, 4.0)
    return base.astype(jnp.bfloat16)


def draw_cache_slots(key, part):
    keys_zero = shared_keys(key)
    key = jax.random.fold_in(key, 5)
    key_width = KV_HEADS * HEAD
    value_scale = 0.25
    rest = jnp.clip(jax.random.normal(key, (N_SECTION, BATCH, SEQ, 2 * key_width), jnp.float32), -4.0, 4.0)
    rest = jnp.concatenate([rest[:, :, :, :key_width], value_scale * rest[:, :, :, key_width:]], axis=3)
    slot_zero = jnp.concatenate([keys_zero, rest[0, :, :, key_width:]], axis=2)
    return rest.at[0].set(slot_zero).astype(jnp.bfloat16)


def draw_segment_ids(key, part):
    key = jax.random.fold_in(key, 3)
    pair_count = SEQ // 2
    start_count = max(1, SEQ // 64)
    row_keys = jax.random.split(key, BATCH)

    def one_row(row_key):
        order = jax.random.permutation(row_key, pair_count - 1)
        chosen = (order < start_count).astype(jnp.int32)
        return jnp.concatenate([jnp.zeros((1,), jnp.int32), chosen])
    starts = jax.vmap(one_row)(row_keys)
    labels = jnp.cumsum(starts, axis=1)
    return jnp.repeat(labels, 2, axis=1).astype(jnp.int32)


def levels(key, shape, pieces, least, high):
    def one(dim, shards_of):
        steps = jax.random.uniform(jax.random.fold_in(jax.random.fold_in(key, 6), dim), (shards_of,), jnp.float32, least / len(pieces), high / len(pieces))
        return jnp.repeat(jnp.exp(steps), shape[dim] // shards_of).reshape((-1,) + (1,) * (len(shape) - dim - 1))

    factor_of = one(*pieces[0])
    for cut in pieces[1:]:
        factor_of = factor_of * one(*cut)
    return factor_of


def noise(key, shape, scale, reach, cuts=(), held_as=jnp.bfloat16):
    entries = jax.random.normal(key, shape, jnp.float32) * scale
    if len(cuts) > 0:
        entries = levels(key, shape, cuts, -0.22, 0.18) * entries
    return jnp.clip(entries, min=-reach, max=reach).astype(held_as)


def setup_inputs(seed: int = 0) -> dict:
    seeds = jax.random.split(jax.random.key(seed), 6)
    saved_inputs = draw_saved_inputs(jax.random.fold_in(seeds[5], 71), 0)
    query_gains = jnp.clip(1.0 + 0.1 * jax.random.normal(seeds[1], (N_SECTION, HEADS * HEAD), jnp.float32), 0.5, 1.5)
    cache_slots = draw_cache_slots(jax.random.fold_in(seeds[5], 71), 0)
    segment_ids = draw_segment_ids(jax.random.fold_in(seeds[5], 71), 0)
    output_grad = noise(seeds[4], (BATCH, SEQ, HEADS * HEAD), 1.0, 6.0, ((0, 16),))
    return dict(saved_inputs=saved_inputs, query_gains=query_gains, cache_slots=cache_slots, segment_ids=segment_ids, output_grad=output_grad)


def layer_backward(saved_rows, gain_row, cache_rows, grad_rows, segment_row):
    length = saved_rows.shape[0]
    key_width = KV_HEADS * HEAD
    group = HEADS // KV_HEADS
    score_scale = HEAD ** -0.5
    queries = (saved_rows.astype(jnp.float32) * gain_row).astype(jnp.bfloat16)
    query_heads = queries.astype(jnp.float32).reshape(length, KV_HEADS, group, HEAD)
    key_heads = cache_rows[:, :key_width].astype(jnp.float32).reshape(length, KV_HEADS, HEAD)
    value_heads = cache_rows[:, key_width:].astype(jnp.float32).reshape(length, KV_HEADS, HEAD)
    grad_heads = grad_rows.astype(jnp.float32).reshape(length, KV_HEADS, group, HEAD)
    scores = jnp.einsum("qkgd,tkd->kgqt", query_heads, key_heads) * score_scale
    position = jnp.arange(length)
    allowed = (position[:, None] >= position[None, :]) & (segment_row[:, None] == segment_row[None, :])
    scores = jnp.where(allowed, scores, -jnp.inf)
    row_max = jnp.max(scores, axis=-1, keepdims=True)
    exp_terms = jnp.exp(scores - row_max)
    attn_probs = exp_terms / jnp.sum(exp_terms, axis=-1, keepdims=True)
    dprob = jnp.einsum("qkgd,tkd->kgqt", grad_heads, value_heads)
    row_delta = jnp.sum(attn_probs * dprob, axis=-1, keepdims=True)
    dscore = attn_probs * (dprob - row_delta)
    probs_round = lax.optimization_barrier(attn_probs.astype(jnp.bfloat16)).astype(jnp.float32)
    dscore_round = lax.optimization_barrier(dscore.astype(jnp.bfloat16)).astype(jnp.float32)
    dvalues = jnp.einsum("kgqt,qkgd->tkd", probs_round, grad_heads)
    dquery = jnp.einsum("kgqt,tkd->qkgd", dscore_round, key_heads) * score_scale
    dkeys = jnp.einsum("kgqt,qkgd->tkd", dscore_round, query_heads) * score_scale
    dquery_flat = dquery.reshape(length, HEADS * HEAD)
    grad_next = (grad_rows.astype(jnp.float32) + gain_row * dquery_flat).astype(jnp.bfloat16)
    gain_part = jnp.sum(dquery_flat * saved_rows.astype(jnp.float32), axis=0)
    cache_part = jnp.concatenate([dkeys.reshape(length, key_width), dvalues.reshape(length, key_width)], axis=1)
    return grad_next, cache_part, gain_part


def reference(saved_inputs, query_gains, cache_slots, segment_ids, output_grad):
    shared_cache = cache_slots[0]
    carried = output_grad
    cache_total = jnp.zeros(shared_cache.shape, jnp.float32)
    grads_list = [None] * N_SECTION
    gains_list = [None] * N_SECTION
    for layer in reversed(range(N_SECTION)):
        gain_row = query_gains[layer]

        def one_micro(items):
            return layer_backward(items[0], gain_row, items[1], items[2], items[3])

        grad_next, cache_part, gain_part = lax.map(one_micro, (saved_inputs[layer], shared_cache, carried, segment_ids))
        cache_total = cache_total + cache_part
        gains_list[layer] = jnp.sum(gain_part, axis=0)
        grads_list[layer] = grad_next
        carried = grad_next
    return jnp.stack(grads_list), cache_total.astype(jnp.bfloat16), jnp.stack(gains_list)
```

```python
import functools

import jax
import jax.numpy as jnp
from jax import lax
from jax.experimental import pallas as pl
from jax.experimental.pallas import tpu as pltpu
from jax.sharding import PartitionSpec as P

HEADS = 20
KV_HEADS = 4
HEAD = 128
GROUP = HEADS // KV_HEADS
WIDE = GROUP * HEAD
SECTIONS = 16
MICROS = 2
LENGTH = 256
BLOCK = 64
LOG2E = 1.4426950408889634
SCALE = HEAD ** -0.5
MASKED = -1e30


def stack_heads(rows):
    return jnp.concatenate([rows[:, h * HEAD : (h + 1) * HEAD] for h in range(GROUP)], axis=0)


def unstack_heads(rows):
    return jnp.concatenate([rows[h * BLOCK : (h + 1) * BLOCK] for h in range(GROUP)], axis=1)


def chain_kernel(saved_ref, gain_ref, kv_ref, bias_ref, top_ref, before_cache, before_gain,
                 grads_ref, cache_ref, gain_part_ref):
    keys_seen = bias_ref.shape[0]
    contract_last = (((1,), (1,)), ((), ()))
    contract_first = (((0,), (0,)), ((), ()))
    cache_ref[...] = before_cache[...]

    def layer(step, incoming):
        s = SECTIONS - 1 - step
        keys = kv_ref[:keys_seen, :HEAD]
        values = kv_ref[:keys_seen, HEAD:]
        gain = gain_ref[pl.ds(s, 1), :]
        saved = saved_ref[s].astype(jnp.float32)
        queries = stack_heads((saved * gain).astype(jnp.bfloat16))
        scores = lax.dot_general(keys, queries, contract_last, preferred_element_type=jnp.float32)
        scores = scores * (SCALE * LOG2E) + bias_ref[...]
        exp_terms = jnp.exp2(scores - jnp.max(scores, axis=0, keepdims=True))
        probs = exp_terms * (1.0 / jnp.sum(exp_terms, axis=0, keepdims=True))
        dprob = lax.dot_general(values, incoming, contract_last, preferred_element_type=jnp.float32)
        delta = jnp.sum(probs * dprob, axis=0, keepdims=True)
        dscore = (probs * (dprob - delta)).astype(jnp.bfloat16)
        dquery = unstack_heads(
            lax.dot_general(dscore, keys, contract_first, preferred_element_type=jnp.float32) * SCALE
        )
        cache_ref[:keys_seen, :HEAD] += SCALE * jnp.dot(dscore, queries, preferred_element_type=jnp.float32)
        cache_ref[:keys_seen, HEAD:] += jnp.dot(
            probs.astype(jnp.bfloat16), incoming, preferred_element_type=jnp.float32
        )
        gain_part_ref[pl.ds(s, 1), :] = before_gain[pl.ds(s, 1), :] + jnp.sum(
            dquery * saved, axis=0, keepdims=True
        )
        grads = (unstack_heads(incoming).astype(jnp.float32) + gain * dquery).astype(jnp.bfloat16)
        grads_ref[s] = grads
        return stack_heads(grads)

    lax.fori_loop(0, SECTIONS, layer, stack_heads(top_ref[...]), unroll=2)


def chain(saved, gains, kv_unit, bias, top, cache_part, gain_part):
    columns = GROUP * BLOCK
    keys_seen = bias.shape[0]
    vmem = pl.BlockSpec(memory_space=pltpu.VMEM)
    return pl.pallas_call(
        chain_kernel,
        out_shape=(
            jax.ShapeDtypeStruct((SECTIONS, BLOCK, WIDE), jnp.bfloat16),
            jax.ShapeDtypeStruct((LENGTH, 2 * HEAD), jnp.float32),
            jax.ShapeDtypeStruct((SECTIONS, WIDE), jnp.float32),
        ),
        in_specs=[vmem] * 7,
        out_specs=(vmem, vmem, vmem),
        compiler_params=pltpu.CompilerParams(vmem_limit_bytes=32 * 1024 * 1024),
        cost_estimate=pl.CostEstimate(
            flops=SECTIONS * 10 * columns * keys_seen * HEAD,
            bytes_accessed=6 * 1024 * 1024,
            transcendentals=SECTIONS * columns * keys_seen,
        ),
    )(saved, gains, kv_unit, bias, top, cache_part, gain_part)


def sent_to(array, axis, pairs):
    return lax.ppermute(array, axis, pairs)


def unit_of_cache(cache, me):
    keys = cache[:, :, : KV_HEADS * HEAD].reshape(MICROS, LENGTH, KV_HEADS, HEAD)
    values = cache[:, :, KV_HEADS * HEAD :].reshape(MICROS, LENGTH, KV_HEADS, HEAD)
    units = jnp.concatenate([keys, values], axis=-1).transpose(0, 2, 1, 3)
    quads = units.reshape(4, 2, LENGTH, 2 * HEAD)
    came = [sent_to(quads[j], "section", [(0, 4 * j)]) for j in (1, 2, 3)]
    pair = jnp.where(me == 0, quads[0], came[0] + came[1] + came[2])
    came = [
        sent_to(pair[j // 2], "section", [(4 * a, 4 * a + j) for a in range(4)]) for j in (1, 2, 3)
    ]
    return jnp.where(me % 4 == 0, pair[0], came[0] + came[1] + came[2])


def bias_of(segments, block, keys_seen):
    rows = lax.dynamic_slice(segments, (block * BLOCK,), (BLOCK,))
    key_pos = jnp.arange(keys_seen)
    query_pos = block * BLOCK + jnp.arange(BLOCK)
    allowed = (key_pos[:, None] <= query_pos[None, :]) & (
        segments[:keys_seen, None] == rows[None, :]
    )
    bias = jnp.where(allowed, 0.0, MASKED).astype(jnp.float32)
    return jnp.tile(bias, (1, GROUP))


def on_device(saved_inputs, query_gains, cache_slots, segment_ids, output_grad):
    me = lax.axis_index("section")
    micro, head, half = me // 8, (me % 8) // 2, me % 2
    exchange = functools.partial(
        lax.all_to_all, axis_name="section", split_axis=0, concat_axis=0, tiled=True
    )
    kv_unit = unit_of_cache(cache_slots[0], me)
    gain_spread = jnp.broadcast_to(
        jnp.pad(query_gains.reshape(1, KV_HEADS, 1, WIDE), ((0, 0), (0, 0), (0, 0), (0, 384))),
        (MICROS, KV_HEADS, 2, WIDE + 384),
    )
    gains = exchange(gain_spread.reshape(SECTIONS, 8, 128)).reshape(SECTIONS, WIDE + 384)[:, :WIDE]
    tiles = saved_inputs.reshape(MICROS, 4, BLOCK, KV_HEADS, WIDE).transpose(0, 3, 1, 2, 4)
    late = jnp.stack([tiles[:, :, 3], tiles[:, :, 2]], axis=2).reshape(SECTIONS, BLOCK, WIDE)
    early = tiles[:, :, :2].reshape(SECTIONS, BLOCK, WIDE)
    late_saved = exchange(late)
    early_saved = exchange(early)

    segments = lax.dynamic_index_in_dim(segment_ids, micro, 0, keepdims=False)
    late_block, early_block = 3 - half, half

    def top_of(block):
        start = (micro, block * BLOCK, head * WIDE)
        return lax.dynamic_slice(output_grad, start, (1, BLOCK, WIDE))[0]

    late_grads, cache_part, gain_part = chain(
        late_saved, gains, kv_unit, bias_of(segments, late_block, LENGTH), top_of(late_block),
        jnp.zeros((LENGTH, 2 * HEAD), jnp.float32), jnp.zeros((SECTIONS, WIDE), jnp.float32),
    )
    late_home = exchange(late_grads)
    early_grads, cache_part, gain_part = chain(
        early_saved, gains, kv_unit, bias_of(segments, early_block, LENGTH // 2), top_of(early_block),
        cache_part, gain_part,
    )
    gain_home = exchange(jnp.pad(gain_part, ((0, 0), (0, 384))).reshape(SECTIONS, 8, 128))
    early_home = exchange(early_grads)

    halves = cache_part.reshape(2, LENGTH // 2, 2 * HEAD)
    theirs = sent_to(
        lax.dynamic_index_in_dim(halves, 1 - half, 0, keepdims=False),
        "section", [(i, i ^ 1) for i in range(SECTIONS)],
    )
    mine = (lax.dynamic_index_in_dim(halves, half, 0, keepdims=False) + theirs).astype(jnp.bfloat16)
    whole = exchange(jnp.broadcast_to(mine[None], (SECTIONS, LENGTH // 2, 2 * HEAD)))
    whole = whole.reshape(MICROS, KV_HEADS, LENGTH, 2, HEAD).transpose(0, 2, 3, 1, 4)
    cache_grad = whole.reshape(MICROS, LENGTH, 2 * KV_HEADS * HEAD)

    gain_sum = gain_home.reshape(MICROS, KV_HEADS, 2, WIDE + 384)[..., :WIDE].sum((0, 2))
    gain_sum = gain_sum.reshape(20, 128)
    for bit in (8, 4, 2, 1):
        gain_sum = gain_sum + sent_to(gain_sum, "dp", [(i, i ^ bit) for i in range(16)])

    late_home = late_home.reshape(MICROS, KV_HEADS, 2, BLOCK, WIDE)
    early_home = early_home.reshape(MICROS, KV_HEADS, 2, BLOCK, WIDE)
    blocks = jnp.stack(
        [early_home[:, :, 0], early_home[:, :, 1], late_home[:, :, 1], late_home[:, :, 0]], axis=1
    )
    layer_out = blocks.transpose(0, 1, 3, 2, 4).reshape(1, MICROS, LENGTH, HEADS * HEAD)
    return (layer_out, cache_grad, gain_sum.reshape(1, HEADS * HEAD))


def solution(mesh):
    return jax.shard_map(
        on_device,
        mesh=mesh,
        in_specs=(
            P("section", "dp", None, None),
            P("section", None),
            P("section", "dp", None, None),
            P("dp", None),
            P("dp", None, None),
        ),
        out_specs=(P("section", "dp", None, None), P("dp", None, None), P("section", None)),
        check_vma=False,
    )
```

```python
import jax
import jax.numpy as jnp
from jax import lax
from jax.experimental import pallas as pl
from jax.experimental.pallas import tpu as pltpu
from jax.sharding import PartitionSpec as P

HEADS = 20
KV_HEADS = 4
HEAD = 128
GROUP = HEADS // KV_HEADS
WIDE = GROUP * HEAD
STACK = GROUP * 64
TAIL = 16
KEY_WIDTH = KV_HEADS * HEAD
SECTIONS = 16
RING = 8
MICROS = 2
LENGTH = 256
BLOCK = 64
LOG2E = 1.4426950408889634
SCALE = HEAD ** -0.5
MASKED = -1e30
RING_ORDER = (4, 3, 5, 2, 6, 1, 7)

VMEM = pl.BlockSpec(memory_space=pltpu.VMEM)
SMEM = pl.BlockSpec(memory_space=pltpu.SMEM)
IN_HBM = pl.BlockSpec(memory_space=pltpu.HBM)


def moved(array, pairs):
    return lax.ppermute(array, "section", pairs)


def turned(array, by):
    return moved(array, [(i, i // RING * RING + (i + by) % RING) for i in range(SECTIONS)])


def swapped(array, bit, axis="section"):
    return lax.ppermute(array, axis, [(i, i ^ bit) for i in range(16)])


def exchange(array):
    return lax.all_to_all(array, "section", 0, 0, tiled=True)


def after(array, *others):
    return lax.optimization_barrier((array, *others))[0]


def run_copies(stages):
    for first, _ in stages:
        first.start()
    for first, later in stages:
        first.wait()
        for copy in later:
            copy.start()
    for _, later in stages:
        for copy in later:
            copy.wait()


def moving_call(kernel, out_shape, scratch, in_specs, aliases=None):
    outs = out_shape if isinstance(out_shape, list) else [out_shape]
    size = sum(2 * out.size * out.dtype.itemsize for out in outs)
    out_specs = [IN_HBM] + [VMEM] * (len(outs) - 1)
    return pl.pallas_call(
        kernel,
        out_shape=out_shape,
        in_specs=in_specs,
        out_specs=out_specs if isinstance(out_shape, list) else IN_HBM,
        input_output_aliases=aliases or {},
        scratch_shapes=scratch,
        compiler_params=pltpu.CompilerParams(vmem_limit_bytes=12 * 1024 * 1024),
        cost_estimate=pl.CostEstimate(flops=0, bytes_accessed=size, transcendentals=0),
    )


def home_places(late):
    for owner in range(SECTIONS):
        micro, head, half = owner // RING, owner % RING // 2, owner % 2
        block = 3 - half if late else half
        yield owner, (micro, pl.ds(block * BLOCK, BLOCK), pl.ds(head * WIDE, WIDE))


def cache_units(cache):
    def kernel(cache_ref, out_ref, held, in_sems, out_sems):
        copies = []
        for unit in range(2 * KV_HEADS):
            micro, head = unit // KV_HEADS, unit % KV_HEADS
            for part in range(2):
                column = part * KEY_WIDTH + head * HEAD
                slot = held.at[unit, part]
                copies.append((
                    pltpu.make_async_copy(
                        cache_ref.at[micro, :, pl.ds(column, HEAD)], slot, in_sems.at[unit, part]
                    ),
                    [pltpu.make_async_copy(
                        slot, out_ref.at[unit, :, pl.ds(part * HEAD, HEAD)],
                        out_sems.at[2 * unit + part],
                    )],
                ))
        run_copies(copies)

    units = 2 * KV_HEADS
    out = jax.ShapeDtypeStruct((units, LENGTH, 2 * HEAD), cache.dtype)
    scratch = [
        pltpu.VMEM((units, 2, LENGTH, HEAD), cache.dtype),
        pltpu.SemaphoreType.DMA((units, 2)),
        pltpu.SemaphoreType.DMA((2 * units,)),
    ]
    return moving_call(kernel, out, scratch, [IN_HBM])(cache)


def cache_whole(me, near, far):
    def kernel(me_ref, near_ref, far_ref, whole_ref, held, in_sems, out_sems):
        here = me_ref[0]
        copies = []
        for side, source in enumerate((near_ref, far_ref)):
            for j in range(RING):
                owner = lax.rem(here + RING - j, RING)
                micro = lax.rem(here // RING + side, 2)
                head, half = owner // 2, lax.rem(owner, 2)
                start = pl.multiple_of(half * (LENGTH // 2), LENGTH // 2)
                later = []
                for part in range(2):
                    column = pl.multiple_of(head * HEAD + part * KEY_WIDTH, HEAD)
                    later.append(
                        pltpu.make_async_copy(
                            held.at[side, j, :, pl.ds(part * HEAD, HEAD)],
                            whole_ref.at[micro, pl.ds(start, LENGTH // 2), pl.ds(column, HEAD)],
                            out_sems.at[(side * RING + j) * 2 + part],
                        )
                    )
                first = pltpu.make_async_copy(source.at[j], held.at[side, j], in_sems.at[side, j])
                copies.append((first, later))
        run_copies(copies)

    out = jax.ShapeDtypeStruct((MICROS, LENGTH, 2 * KEY_WIDTH), near.dtype)
    scratch = [
        pltpu.VMEM((2,) + near.shape, near.dtype),
        pltpu.SemaphoreType.DMA((2, RING)),
        pltpu.SemaphoreType.DMA((4 * RING,)),
    ]
    return moving_call(kernel, out, scratch, [SMEM, IN_HBM, IN_HBM])(me.reshape(1), near, far)


def stack_heads(rows):
    return jnp.concatenate([rows[:, h * HEAD : (h + 1) * HEAD] for h in range(GROUP)], axis=0)


def unstack_heads(rows):
    return jnp.concatenate([rows[h * BLOCK : (h + 1) * BLOCK] for h in range(GROUP)], axis=1)


def three_parts(rows):
    parts = []
    for i in range(GROUP):
        left = rows[i : i + 1]
        for _ in range(3):
            part = left.astype(jnp.bfloat16).astype(jnp.float32)
            parts.append(part)
            left = left - part
    parts.append(jnp.zeros_like(parts[0]))
    return jnp.concatenate(parts, axis=0).astype(jnp.bfloat16)


def from_parts(parts):
    parts = parts.astype(jnp.float32)
    return jnp.concatenate(
        [
            parts[3 * i : 3 * i + 1] + parts[3 * i + 1 : 3 * i + 2] + parts[3 * i + 2 : 3 * i + 3]
            for i in range(GROUP)
        ],
        axis=0,
    )


def pack(whole, late, gains=None):
    tall = STACK if gains is None else STACK + TAIL

    def kernel(*refs):
        whole_ref, (out_ref, held, stacked, in_sems, out_sems) = refs[-6], refs[-5:]
        arriving = [
            pltpu.make_async_copy(whole_ref.at[place], held.at[owner], in_sems.at[owner])
            for owner, place in home_places(late)
        ]
        for copy in arriving:
            copy.start()
        leaving = []
        for owner in range(SECTIONS):
            if gains is not None:
                first = owner % RING // 2 * GROUP
                stacked[owner, STACK:] = three_parts(refs[0][first : first + GROUP])
            arriving[owner].wait()
            for h in range(GROUP):
                stacked[owner, h * BLOCK : (h + 1) * BLOCK] = held[owner, :, h * HEAD : (h + 1) * HEAD]
            copy = pltpu.make_async_copy(stacked.at[owner], out_ref.at[owner], out_sems.at[owner])
            copy.start()
            leaving.append(copy)
        for copy in leaving:
            copy.wait()

    out = jax.ShapeDtypeStruct((SECTIONS, tall, HEAD), whole.dtype)
    scratch = [
        pltpu.VMEM((SECTIONS, BLOCK, WIDE), whole.dtype),
        pltpu.VMEM(out.shape, whole.dtype),
        pltpu.SemaphoreType.DMA((SECTIONS,)),
        pltpu.SemaphoreType.DMA((SECTIONS,)),
    ]
    if gains is None:
        return moving_call(kernel, out, scratch, [IN_HBM])(whole)
    return moving_call(kernel, out, scratch, [VMEM, IN_HBM])(gains, whole)


def unpack(came, late, whole=None):
    tall = came.shape[1]

    def kernel(came_ref, *rest):
        if whole is None:
            out_ref, (held, spread, in_sems, out_sems) = rest[0], rest[1:]
        else:
            _, out_ref, gain_ref, held, spread, in_sems, out_sems = rest
        arriving = [
            pltpu.make_async_copy(came_ref.at[owner], held.at[owner], in_sems.at[owner])
            for owner in range(SECTIONS)
        ]
        for copy in arriving:
            copy.start()
        leaving = []
        for owner, place in home_places(late):
            arriving[owner].wait()
            for h in range(GROUP):
                spread[owner, :, h * HEAD : (h + 1) * HEAD] = held[owner, h * BLOCK : (h + 1) * BLOCK]
            copy = pltpu.make_async_copy(spread.at[owner], out_ref.at[place], out_sems.at[owner])
            copy.start()
            leaving.append(copy)
        if whole is not None:
            for head in range(KV_HEADS):
                total = jnp.zeros((GROUP, HEAD), jnp.float32)
                for owner in (2 * head, 2 * head + 1, RING + 2 * head, RING + 2 * head + 1):
                    total += from_parts(held[owner, STACK:])
                gain_ref[head * GROUP : (head + 1) * GROUP] = total
        for copy in leaving:
            copy.wait()

    out = jax.ShapeDtypeStruct((MICROS, LENGTH, HEADS * HEAD), came.dtype)
    scratch = [
        pltpu.VMEM(came.shape, came.dtype),
        pltpu.VMEM((SECTIONS, BLOCK, WIDE), came.dtype),
        pltpu.SemaphoreType.DMA((SECTIONS,)),
        pltpu.SemaphoreType.DMA((SECTIONS,)),
    ]
    if whole is None:
        return moving_call(kernel, out, scratch, [IN_HBM])(came)
    outs = [out, jax.ShapeDtypeStruct((HEADS, HEAD), jnp.float32)]
    return moving_call(kernel, outs, scratch, [IN_HBM, IN_HBM], {1: 0})(came, whole)


def with_gains(grads, gain_part):
    def kernel(gain_ref, _, out_ref, tails, sems):
        copies = []
        for s in range(SECTIONS):
            tails[s] = three_parts(gain_ref[s])
            copy = pltpu.make_async_copy(tails.at[s], out_ref.at[s, pl.ds(STACK, TAIL)], sems.at[s])
            copy.start()
            copies.append(copy)
        for copy in copies:
            copy.wait()

    out = jax.ShapeDtypeStruct(grads.shape, grads.dtype)
    scratch = [
        pltpu.VMEM((SECTIONS, TAIL, HEAD), grads.dtype),
        pltpu.SemaphoreType.DMA((SECTIONS,)),
    ]
    return moving_call(kernel, out, scratch, [VMEM, IN_HBM], {1: 0})(gain_part, grads)


def per_row(gains):
    return jnp.concatenate(
        [jnp.broadcast_to(gains[h : h + 1], (BLOCK, HEAD)) for h in range(GROUP)], axis=0
    )


def per_head(rows):
    sums = [
        jnp.sum(rows[h * BLOCK : (h + 1) * BLOCK], axis=0, keepdims=True) for h in range(GROUP)
    ]
    return jnp.concatenate(sums + [jnp.zeros((8 - GROUP, HEAD), jnp.float32)], axis=0)


def run_layers(saved_ref, gain_of, kv_ref, bias_ref, top_ref, grads_ref, cache_ref, add_gain):
    seen = bias_ref.shape[0]
    contract_last = (((1,), (1,)), ((), ()))
    contract_first = (((0,), (0,)), ((), ()))

    def layer(step, incoming):
        s = SECTIONS - 1 - step
        keys, values = kv_ref[:seen, :HEAD], kv_ref[:seen, HEAD:]
        gain = per_row(gain_of(s))
        saved = saved_ref[s, :STACK].astype(jnp.float32)
        queries = (saved * gain).astype(jnp.bfloat16)
        scores = lax.dot_general(keys, queries, contract_last, preferred_element_type=jnp.float32)
        scores = scores * (SCALE * LOG2E) + bias_ref[...]
        exp_terms = jnp.exp2(scores - jnp.max(scores, axis=0, keepdims=True))
        probs = exp_terms * (1.0 / jnp.sum(exp_terms, axis=0, keepdims=True))
        dprob = lax.dot_general(values, incoming, contract_last, preferred_element_type=jnp.float32)
        delta = jnp.sum(probs * dprob, axis=0, keepdims=True)
        dscore = (probs * (dprob - delta)).astype(jnp.bfloat16)
        dquery = SCALE * lax.dot_general(
            dscore, keys, contract_first, preferred_element_type=jnp.float32
        )
        cache_ref[:seen, :HEAD] += SCALE * jnp.dot(dscore, queries, preferred_element_type=jnp.float32)
        cache_ref[:seen, HEAD:] += jnp.dot(
            probs.astype(jnp.bfloat16), incoming, preferred_element_type=jnp.float32
        )
        add_gain(s, per_head(dquery * saved))
        grads = (incoming.astype(jnp.float32) + gain * dquery).astype(jnp.bfloat16)
        grads_ref[s, :STACK] = grads
        return grads

    top = jnp.concatenate([top_ref[:, h * HEAD : (h + 1) * HEAD] for h in range(GROUP)], axis=0)
    lax.fori_loop(0, SECTIONS, layer, top, unroll=2)


def late_kernel(saved_ref, kv_ref, bias_ref, top_ref, grads_ref, cache_ref, gain_ref, part_ref):
    for s in range(SECTIONS):
        gain_ref[s, :GROUP] = from_parts(saved_ref[s, STACK:])
    cache_ref[...] = jnp.zeros_like(cache_ref)

    def add_gain(s, part):
        part_ref[s] = part

    run_layers(
        saved_ref, lambda s: gain_ref[s], kv_ref, bias_ref, top_ref, grads_ref, cache_ref, add_gain
    )


def early_kernel(saved_ref, kv_ref, bias_ref, top_ref, cache_before, gain_ref, part_before,
                 grads_ref, cache_ref, part_ref):
    cache_ref[...] = cache_before[...]

    def add_gain(s, part):
        part_ref[s] = part_before[s] + part

    run_layers(
        saved_ref, lambda s: gain_ref[s], kv_ref, bias_ref, top_ref, grads_ref, cache_ref, add_gain
    )


def chain(kernel, saved, kv_unit, bias, top, grads_tall, *before):
    seen, columns = bias.shape
    shapes = [
        ((SECTIONS, grads_tall, HEAD), jnp.bfloat16),
        ((LENGTH, 2 * HEAD), jnp.float32),
        ((SECTIONS, 8, HEAD), jnp.float32),
    ]
    if not before:
        shapes.append(shapes[-1])
    return pl.pallas_call(
        kernel,
        out_shape=[jax.ShapeDtypeStruct(*shape) for shape in shapes],
        in_specs=[VMEM] * (4 + len(before)),
        out_specs=[VMEM] * len(shapes),
        compiler_params=pltpu.CompilerParams(vmem_limit_bytes=24 * 1024 * 1024),
        cost_estimate=pl.CostEstimate(
            flops=SECTIONS * 10 * columns * seen * HEAD,
            bytes_accessed=6 * 1024 * 1024,
            transcendentals=SECTIONS * columns * seen,
        ),
    )(saved, kv_unit, bias, top, *before)


def bias_of(segments, block, keys_seen):
    rows = lax.dynamic_slice(segments, (block * BLOCK,), (BLOCK,))
    key_pos = jnp.arange(keys_seen)
    query_pos = block * BLOCK + jnp.arange(BLOCK)
    allowed = (key_pos[:, None] <= query_pos[None, :]) & (
        segments[:keys_seen, None] == rows[None, :]
    )
    bias = jnp.where(allowed, 0.0, MASKED).astype(jnp.float32)
    return jnp.tile(bias, (1, GROUP))


def on_device(saved_inputs, query_gains, cache_slots, segment_ids, output_grad):
    me = lax.axis_index("section")
    micro, head, half = me // RING, me % RING // 2, me % 2

    units = cache_units(cache_slots[0])
    across = moved(units[KV_HEADS:], [(0, RING)])
    late_packed = pack(saved_inputs[0], True, query_gains.reshape(HEADS, HEAD))
    late_saved = exchange(after(late_packed, across))
    four = jnp.where(me < RING, units[:KV_HEADS], across)
    came = [moved(four[k], [(0, 2 * k), (RING, RING + 2 * k)]) for k in (2, 1, 3)]
    at_even = jnp.where(me % RING == 0, four[0], came[0] + came[1] + came[2])
    at_odd = moved(at_even, [(i, i + 1) for i in range(0, SECTIONS, 2)])
    kv_unit = jnp.where(half == 0, at_even, at_odd)
    early_packed = after(pack(saved_inputs[0], False), late_saved, at_odd)
    early_saved = exchange(early_packed)

    segments = lax.dynamic_index_in_dim(segment_ids, micro, 0, keepdims=False)
    late_block, early_block = 3 - half, half

    def top_of(block):
        start = (micro, block * BLOCK, head * WIDE)
        return lax.dynamic_slice(output_grad, start, (1, BLOCK, WIDE))[0]

    late_grads, cache_part, gains, gain_part = chain(
        late_kernel, late_saved, kv_unit, bias_of(segments, late_block, LENGTH),
        top_of(late_block), STACK,
    )
    late_home = exchange(late_grads)
    early_grads, cache_part, gain_part = chain(
        early_kernel, early_saved, kv_unit, bias_of(segments, early_block, LENGTH // 2),
        top_of(early_block), STACK + TAIL, cache_part, gains, gain_part,
    )
    halves = cache_part.reshape(2, LENGTH // 2, 2 * HEAD)
    theirs = swapped(lax.dynamic_index_in_dim(halves, 1 - half, 0, keepdims=False), 1)
    for bit in (1, 2, 4, 8):
        gain_part = gain_part + swapped(gain_part, bit, "dp")
    early_grads = with_gains(early_grads, gain_part)

    mine = lax.dynamic_index_in_dim(halves, half, 0, keepdims=False) + theirs
    mine = after(mine.astype(jnp.bfloat16), early_grads)
    ring = {0: mine}
    for r in RING_ORDER:
        ring[r] = turned(mine, r)
    early_home = exchange(after(early_grads, late_home, *(ring[r] for r in RING_ORDER)))
    whole = unpack(late_home, True)
    near = jnp.stack([ring[r] for r in range(RING)])
    cache_grad = cache_whole(me, near, swapped(near, RING))
    layer_out, gain_sum = unpack(early_home, False, whole)
    return (layer_out[None], cache_grad, gain_sum.reshape(1, HEADS * HEAD))


def solution(mesh):
    return jax.shard_map(
        on_device,
        mesh=mesh,
        in_specs=(
            P("section", "dp", None, None),
            P("section", None),
            P("section", "dp", None, None),
            P("dp", None),
            P("dp", None, None),
        ),
        out_specs=(P("section", "dp", None, None), P("dp", None, None), P("section", None)),
        check_vma=False,
    )
```

```python
import jax
import jax.numpy as jnp
from jax import lax
from jax.experimental import pallas as pl
from jax.experimental.pallas import tpu as pltpu
from jax.sharding import PartitionSpec as P

HEADS = 20
KV_HEADS = 4
HEAD = 128
GROUP = HEADS // KV_HEADS
WIDE = GROUP * HEAD
STACK = GROUP * 64
TAIL = 16
KEY_WIDTH = KV_HEADS * HEAD
SECTIONS = 16
RING = 8
MICROS = 2
LENGTH = 256
BLOCK = 64
LOG2E = 1.4426950408889634
SCALE = HEAD ** -0.5
MASKED = -1e30
RING_ORDER = (4, 3, 5, 2, 6, 1, 7)
UNITS_FLOPS = 40_000_000_000
ALL_ROOM = 56 * 1024 * 1024
SOME_ROOM = 12 * 1024 * 1024
GATHERED = ((0, 4), (1, 5), (7, 3), (2,), (6,))

VMEM = pl.BlockSpec(memory_space=pltpu.VMEM)
SMEM = pl.BlockSpec(memory_space=pltpu.SMEM)
IN_HBM = pl.BlockSpec(memory_space=pltpu.HBM)


def moved(array, pairs):
    return lax.ppermute(array, "section", pairs)


def turned(array, by):
    return moved(array, [(i, i // RING * RING + (i + by) % RING) for i in range(SECTIONS)])


def swapped(array, bit, axis="section"):
    return lax.ppermute(array, axis, [(i, i ^ bit) for i in range(16)])


def exchange(array):
    return lax.all_to_all(array, "section", 0, 0, tiled=True)


def after(array, *others):
    return lax.optimization_barrier((array, *others))[0]


def run_copies(stages):
    for first, _ in stages:
        first.start()
    for first, later in stages:
        first.wait()
        for copy in later:
            copy.start()
    for _, later in stages:
        for copy in later:
            copy.wait()


def moving_call(kernel, out_shape, scratch, in_specs, aliases=None, room=SOME_ROOM):
    outs = out_shape if isinstance(out_shape, list) else [out_shape]
    size = sum(2 * out.size * out.dtype.itemsize for out in outs)
    out_specs = [IN_HBM] + [VMEM] * (len(outs) - 1)
    return pl.pallas_call(
        kernel,
        out_shape=out_shape,
        in_specs=in_specs,
        out_specs=out_specs if isinstance(out_shape, list) else IN_HBM,
        input_output_aliases=aliases or {},
        scratch_shapes=scratch,
        compiler_params=pltpu.CompilerParams(vmem_limit_bytes=room),
        cost_estimate=pl.CostEstimate(flops=0, bytes_accessed=size, transcendentals=0),
    )


def home_places(late):
    for owner in range(SECTIONS):
        micro, head, half = owner // RING, owner % RING // 2, owner % 2
        block = 3 - half if late else half
        yield owner, (micro, pl.ds(block * BLOCK, BLOCK), pl.ds(head * WIDE, WIDE))


def own_units(me, raw, across):
    def kernel(me_ref, raw_ref, across_ref, *rest):
        out_refs, (held, in_sems, out_sems) = rest[:KV_HEADS], rest[KV_HEADS:]

        def take(source):
            copies = []
            for head in range(KV_HEADS):
                for part in range(2):
                    column = part * KEY_WIDTH + head * HEAD
                    slot = held.at[head, part]
                    copies.append((
                        pltpu.make_async_copy(
                            source.at[:, pl.ds(column, HEAD)], slot, in_sems.at[head, part]
                        ),
                        [pltpu.make_async_copy(
                            slot, out_refs[head].at[:, pl.ds(part * HEAD, HEAD)],
                            out_sems.at[head, part],
                        )],
                    ))
            run_copies(copies)

        pl.when(me_ref[0] < RING)(lambda: take(raw_ref.at[0]))
        pl.when(me_ref[0] >= RING)(lambda: take(across_ref))

    return pl.pallas_call(
        kernel,
        out_shape=[jax.ShapeDtypeStruct((LENGTH, 2 * HEAD), raw.dtype)] * KV_HEADS,
        in_specs=[SMEM, IN_HBM, IN_HBM],
        out_specs=[IN_HBM] * KV_HEADS,
        scratch_shapes=[
            pltpu.VMEM((KV_HEADS, 2, LENGTH, HEAD), raw.dtype),
            pltpu.SemaphoreType.DMA((KV_HEADS, 2)),
            pltpu.SemaphoreType.DMA((KV_HEADS, 2)),
        ],
        compiler_params=pltpu.CompilerParams(vmem_limit_bytes=SOME_ROOM),
        cost_estimate=pl.CostEstimate(
            flops=UNITS_FLOPS, bytes_accessed=1024 * 1024, transcendentals=0
        ),
    )(me.reshape(1), raw, across)


def cache_whole(me, *pieces):
    def kernel(me_ref, *refs):
        sources, (whole_ref, held, in_sems, out_sems) = refs[: len(GATHERED)], refs[len(GATHERED) :]
        here = me_ref[0]
        copies = []
        n = 0
        for source, places in zip(sources, GATHERED):
            later = []
            first_slot = n
            for i, back in enumerate(places):
                for side in range(2):
                    owner = lax.rem(here + RING - back, RING)
                    micro = lax.rem(here // RING + side, 2)
                    head, half = owner // 2, lax.rem(owner, 2)
                    start = pl.multiple_of(half * (LENGTH // 2), LENGTH // 2)
                    for part in range(2):
                        column = pl.multiple_of(head * HEAD + part * KEY_WIDTH, HEAD)
                        later.append(
                            pltpu.make_async_copy(
                                held.at[n, :, pl.ds(part * HEAD, HEAD)],
                                whole_ref.at[micro, pl.ds(start, LENGTH // 2), pl.ds(column, HEAD)],
                                out_sems.at[n, part],
                            )
                        )
                    n += 1
            slots = held.at[pl.ds(first_slot, n - first_slot)]
            copies.append((pltpu.make_async_copy(source, slots, in_sems.at[first_slot]), later))
        run_copies(copies)

    out = jax.ShapeDtypeStruct((MICROS, LENGTH, 2 * KEY_WIDTH), pieces[0].dtype)
    scratch = [
        pltpu.VMEM((SECTIONS, LENGTH // 2, 2 * HEAD), out.dtype),
        pltpu.SemaphoreType.DMA((SECTIONS,)),
        pltpu.SemaphoreType.DMA((SECTIONS, 2)),
    ]
    in_specs = [SMEM] + [IN_HBM] * len(pieces)
    return moving_call(kernel, out, scratch, in_specs)(me.reshape(1), *pieces)


def three_parts(rows):
    parts = []
    for i in range(GROUP):
        left = rows[i : i + 1]
        for _ in range(3):
            part = left.astype(jnp.bfloat16).astype(jnp.float32)
            parts.append(part)
            left = left - part
    parts.append(jnp.zeros_like(parts[0]))
    return jnp.concatenate(parts, axis=0).astype(jnp.bfloat16)


def from_parts(parts):
    parts = parts.astype(jnp.float32)
    return jnp.concatenate(
        [
            parts[3 * i : 3 * i + 1] + parts[3 * i + 1 : 3 * i + 2] + parts[3 * i + 2 : 3 * i + 3]
            for i in range(GROUP)
        ],
        axis=0,
    )


def pack(whole, late, gains=None):
    tall = STACK if gains is None else STACK + TAIL

    def kernel(*refs):
        whole_ref, (out_ref, held, stacked, in_sems, out_sems) = refs[-6], refs[-5:]
        arriving = [
            pltpu.make_async_copy(whole_ref.at[place], held.at[owner], in_sems.at[owner])
            for owner, place in home_places(late)
        ]
        for copy in arriving:
            copy.start()
        leaving = []
        for owner in range(SECTIONS):
            if gains is not None:
                first = owner % RING // 2 * WIDE
                heads = [refs[0][:, first + h * HEAD : first + (h + 1) * HEAD] for h in range(GROUP)]
                stacked[owner, STACK:] = three_parts(jnp.concatenate(heads, axis=0))
            arriving[owner].wait()
            for h in range(GROUP):
                stacked[owner, h * BLOCK : (h + 1) * BLOCK] = held[owner, :, h * HEAD : (h + 1) * HEAD]
            copy = pltpu.make_async_copy(stacked.at[owner], out_ref.at[owner], out_sems.at[owner])
            copy.start()
            leaving.append(copy)
        for copy in leaving:
            copy.wait()

    out = jax.ShapeDtypeStruct((SECTIONS, tall, HEAD), whole.dtype)
    scratch = [
        pltpu.VMEM((SECTIONS, BLOCK, WIDE), whole.dtype),
        pltpu.VMEM(out.shape, whole.dtype),
        pltpu.SemaphoreType.DMA((SECTIONS,)),
        pltpu.SemaphoreType.DMA((SECTIONS,)),
    ]
    if gains is None:
        return moving_call(kernel, out, scratch, [IN_HBM], room=ALL_ROOM)(whole)
    return moving_call(kernel, out, scratch, [VMEM, IN_HBM], room=ALL_ROOM)(gains, whole)


def unpack(came, late, whole=None):
    tall = came.shape[1]

    def kernel(came_ref, *rest):
        if whole is None:
            out_ref, (held, spread, in_sems, out_sems) = rest[0], rest[1:]
        else:
            _, out_ref, gain_ref, held, spread, in_sems, out_sems = rest
        arriving = [
            pltpu.make_async_copy(came_ref.at[owner], held.at[owner], in_sems.at[owner])
            for owner in range(SECTIONS)
        ]
        for copy in arriving:
            copy.start()
        leaving = []
        for owner, place in home_places(late):
            arriving[owner].wait()
            for h in range(GROUP):
                spread[owner, :, h * HEAD : (h + 1) * HEAD] = held[owner, h * BLOCK : (h + 1) * BLOCK]
            copy = pltpu.make_async_copy(spread.at[owner], out_ref.at[place], out_sems.at[owner])
            copy.start()
            leaving.append(copy)
        if whole is not None:
            for head in range(KV_HEADS):
                total = jnp.zeros((GROUP, HEAD), jnp.float32)
                for owner in (2 * head, 2 * head + 1, RING + 2 * head, RING + 2 * head + 1):
                    total += from_parts(held[owner, STACK:])
                for h in range(GROUP):
                    first = head * WIDE + h * HEAD
                    gain_ref[:, first : first + HEAD] = total[h : h + 1]
        for copy in leaving:
            copy.wait()

    out = jax.ShapeDtypeStruct((MICROS, LENGTH, HEADS * HEAD), came.dtype)
    scratch = [
        pltpu.VMEM(came.shape, came.dtype),
        pltpu.VMEM((SECTIONS, BLOCK, WIDE), came.dtype),
        pltpu.SemaphoreType.DMA((SECTIONS,)),
        pltpu.SemaphoreType.DMA((SECTIONS,)),
    ]
    if whole is None:
        return moving_call(kernel, out, scratch, [IN_HBM])(came)
    outs = [out, jax.ShapeDtypeStruct((1, HEADS * HEAD), jnp.float32)]
    return moving_call(kernel, outs, scratch, [IN_HBM, IN_HBM], {1: 0})(came, whole)


def with_gains(grads, gain_part):
    def kernel(gain_ref, _, out_ref, tails, sems):
        copies = []
        for s in range(SECTIONS):
            tails[s] = three_parts(gain_ref[s])
            copy = pltpu.make_async_copy(tails.at[s], out_ref.at[s, pl.ds(STACK, TAIL)], sems.at[s])
            copy.start()
            copies.append(copy)
        for copy in copies:
            copy.wait()

    out = jax.ShapeDtypeStruct(grads.shape, grads.dtype)
    scratch = [
        pltpu.VMEM((SECTIONS, TAIL, HEAD), grads.dtype),
        pltpu.SemaphoreType.DMA((SECTIONS,)),
    ]
    return moving_call(kernel, out, scratch, [VMEM, IN_HBM], {1: 0})(gain_part, grads)


def per_row(gains):
    return jnp.concatenate(
        [jnp.broadcast_to(gains[h : h + 1], (BLOCK, HEAD)) for h in range(GROUP)], axis=0
    )


def per_head(rows):
    sums = [
        jnp.sum(rows[h * BLOCK : (h + 1) * BLOCK], axis=0, keepdims=True) for h in range(GROUP)
    ]
    return jnp.concatenate(sums + [jnp.zeros((8 - GROUP, HEAD), jnp.float32)], axis=0)


def run_layers(saved_ref, gain_of, kv_ref, bias_ref, top_ref, grads_ref, cache_ref, add_gain):
    seen = bias_ref.shape[0]
    contract_last = (((1,), (1,)), ((), ()))
    contract_first = (((0,), (0,)), ((), ()))

    def layer(step, incoming):
        s = SECTIONS - 1 - step
        keys, values = kv_ref[:seen, :HEAD], kv_ref[:seen, HEAD:]
        gain = per_row(gain_of(s))
        saved = saved_ref[s, :STACK].astype(jnp.float32)
        queries = (saved * gain).astype(jnp.bfloat16)
        scores = lax.dot_general(keys, queries, contract_last, preferred_element_type=jnp.float32)
        scores = scores * (SCALE * LOG2E) + bias_ref[...]
        exp_terms = jnp.exp2(scores - jnp.max(scores, axis=0, keepdims=True))
        probs = exp_terms * (1.0 / jnp.sum(exp_terms, axis=0, keepdims=True))
        dprob = lax.dot_general(values, incoming, contract_last, preferred_element_type=jnp.float32)
        delta = jnp.sum(probs * dprob, axis=0, keepdims=True)
        dscore = (probs * (dprob - delta)).astype(jnp.bfloat16)
        dquery = SCALE * lax.dot_general(
            dscore, keys, contract_first, preferred_element_type=jnp.float32
        )
        cache_ref[:seen, :HEAD] += SCALE * jnp.dot(dscore, queries, preferred_element_type=jnp.float32)
        cache_ref[:seen, HEAD:] += jnp.dot(
            probs.astype(jnp.bfloat16), incoming, preferred_element_type=jnp.float32
        )
        add_gain(s, per_head(dquery * saved))
        grads = (incoming.astype(jnp.float32) + gain * dquery).astype(jnp.bfloat16)
        grads_ref[s, :STACK] = grads
        return grads

    top = jnp.concatenate([top_ref[:, h * HEAD : (h + 1) * HEAD] for h in range(GROUP)], axis=0)
    lax.fori_loop(0, SECTIONS, layer, top, unroll=2)


def late_kernel(saved_ref, kv_ref, bias_ref, top_ref, grads_ref, cache_ref, gain_ref, part_ref):
    for s in range(SECTIONS):
        gain_ref[s, :GROUP] = from_parts(saved_ref[s, STACK:])
    cache_ref[...] = jnp.zeros_like(cache_ref)

    def add_gain(s, part):
        part_ref[s] = part

    run_layers(
        saved_ref, lambda s: gain_ref[s], kv_ref, bias_ref, top_ref, grads_ref, cache_ref, add_gain
    )


def early_kernel(saved_ref, kv_ref, bias_ref, top_ref, cache_before, gain_ref, part_before,
                 grads_ref, cache_ref, part_ref):
    cache_ref[...] = cache_before[...]

    def add_gain(s, part):
        part_ref[s] = part_before[s] + part

    run_layers(
        saved_ref, lambda s: gain_ref[s], kv_ref, bias_ref, top_ref, grads_ref, cache_ref, add_gain
    )


def chain(kernel, saved, kv_unit, bias, top, grads_tall, *before):
    seen, columns = bias.shape
    shapes = [
        ((SECTIONS, grads_tall, HEAD), jnp.bfloat16),
        ((LENGTH, 2 * HEAD), jnp.float32),
        ((SECTIONS, 8, HEAD), jnp.float32),
    ]
    if not before:
        shapes.append(shapes[-1])
    return pl.pallas_call(
        kernel,
        out_shape=[jax.ShapeDtypeStruct(*shape) for shape in shapes],
        in_specs=[VMEM] * (4 + len(before)),
        out_specs=[VMEM] * len(shapes),
        compiler_params=pltpu.CompilerParams(vmem_limit_bytes=ALL_ROOM if not before else 24 * 1024 * 1024),
        cost_estimate=pl.CostEstimate(
            flops=SECTIONS * 10 * columns * seen * HEAD,
            bytes_accessed=6 * 1024 * 1024,
            transcendentals=SECTIONS * columns * seen,
        ),
    )(saved, kv_unit, bias, top, *before)


def bias_of(segments, block, keys_seen):
    rows = lax.dynamic_slice(segments, (block * BLOCK,), (BLOCK,))
    key_pos = jnp.arange(keys_seen)
    query_pos = block * BLOCK + jnp.arange(BLOCK)
    allowed = (key_pos[:, None] <= query_pos[None, :]) & (
        segments[:keys_seen, None] == rows[None, :]
    )
    bias = jnp.where(allowed, 0.0, MASKED).astype(jnp.float32)
    return jnp.tile(bias, (1, GROUP))


def on_device(saved_inputs, query_gains, cache_slots, segment_ids, output_grad):
    me = lax.axis_index("section")
    micro, head, half = me // RING, me % RING // 2, me % 2

    raw = cache_slots[0]
    across = moved(raw[1], [(0, RING)])
    late_saved = exchange(pack(saved_inputs[0], True, query_gains))
    early_packed = pack(saved_inputs[0], False)
    four = own_units(me, raw, across)
    came = [moved(four[k], [(0, 2 * k), (RING, RING + 2 * k)]) for k in (2, 1, 3)]
    at_even = jnp.where(me % RING == 0, four[0], came[0] + came[1] + came[2])
    at_even = after(at_even, early_packed)
    at_odd = moved(at_even, [(i, i + 1) for i in range(0, SECTIONS, 2)])
    kv_unit = jnp.where(half == 0, at_even, at_odd)
    early_saved = exchange(after(early_packed, late_saved, at_odd))

    segments = lax.dynamic_index_in_dim(segment_ids, micro, 0, keepdims=False)
    late_block, early_block = 3 - half, half

    def top_of(block):
        start = (micro, block * BLOCK, head * WIDE)
        return lax.dynamic_slice(output_grad, start, (1, BLOCK, WIDE))[0]

    late_grads, cache_part, gains, gain_part = chain(
        late_kernel, late_saved, kv_unit, bias_of(segments, late_block, LENGTH),
        top_of(late_block), STACK,
    )
    late_home = exchange(late_grads)
    early_grads, cache_part, gain_part = chain(
        early_kernel, early_saved, kv_unit, bias_of(segments, early_block, LENGTH // 2),
        top_of(early_block), STACK + TAIL, cache_part, gains, gain_part,
    )
    halves = cache_part.reshape(2, LENGTH // 2, 2 * HEAD)
    theirs = swapped(lax.dynamic_index_in_dim(halves, 1 - half, 0, keepdims=False), 1)
    for bit in (1, 2, 4, 8):
        gain_part = gain_part + swapped(gain_part, bit, "dp")
    early_grads = with_gains(early_grads, gain_part)

    early_home = exchange(after(early_grads, late_home, theirs))
    mine = lax.dynamic_index_in_dim(halves, half, 0, keepdims=False) + theirs
    mine = after(mine.astype(jnp.bfloat16), early_grads)
    came = [swapped(mine, bit) for bit in (4, 12, 8)]
    whole = unpack(late_home, True)
    here = jnp.stack([mine, came[2]])
    both = jnp.stack([mine, came[2], came[0], came[1]])
    both, here = lax.optimization_barrier((both, here, whole, early_home))[:2]
    pieces = [both, turned(both, 1), turned(both, -1), turned(here, 2), turned(here, -2)]
    cache_grad = cache_whole(me, *pieces)
    layer_out, gain_sum = unpack(early_home, False, whole)
    return (layer_out[None], cache_grad, gain_sum)


def solution(mesh):
    return jax.shard_map(
        on_device,
        mesh=mesh,
        in_specs=(
            P("section", "dp", None, None),
            P("section", None),
            P("section", "dp", None, None),
            P("dp", None),
            P("dp", None, None),
        ),
        out_specs=(P("section", "dp", None, None), P("dp", None, None), P("section", None)),
        check_vma=False,
    )
```

```python
import jax
import jax.numpy as jnp
from jax import lax
from jax.experimental import pallas as pl
from jax.experimental.pallas import tpu as pltpu
from jax.sharding import PartitionSpec as P

HEADS = 20
KV_HEADS = 4
HEAD = 128
GROUP = HEADS // KV_HEADS
WIDE = GROUP * HEAD
STACK = GROUP * 64
TAIL = 16
KEY_WIDTH = KV_HEADS * HEAD
SECTIONS = 16
RING = 8
MICROS = 2
LENGTH = 256
BLOCK = 64
LOG2E = 1.4426950408889634
SCALE = HEAD ** -0.5
MASKED = -1e30
RING_ORDER = (4, 3, 5, 2, 6, 1, 7)
UNITS_FLOPS = 40_000_000_000
ALL_ROOM = 56 * 1024 * 1024
SOME_ROOM = 12 * 1024 * 1024
GATHERED = ((0, 4), (1, 5), (7, 3), (2,), (6,))

VMEM = pl.BlockSpec(memory_space=pltpu.VMEM)
SMEM = pl.BlockSpec(memory_space=pltpu.SMEM)
IN_HBM = pl.BlockSpec(memory_space=pltpu.HBM)


def moved(array, pairs):
    return lax.ppermute(array, "section", pairs)


def turned(array, by):
    return moved(array, [(i, i // RING * RING + (i + by) % RING) for i in range(SECTIONS)])


def swapped(array, bit, axis="section"):
    return lax.ppermute(array, axis, [(i, i ^ bit) for i in range(16)])


def exchange(array):
    return lax.all_to_all(array, "section", 0, 0, tiled=True)


def after(array, *others):
    return lax.optimization_barrier((array, *others))[0]


def run_copies(stages):
    for first, _ in stages:
        first.start()
    for first, later in stages:
        first.wait()
        for copy in later:
            copy.start()
    for _, later in stages:
        for copy in later:
            copy.wait()


def moving_call(kernel, out_shape, scratch, in_specs, aliases=None, room=SOME_ROOM):
    outs = out_shape if isinstance(out_shape, list) else [out_shape]
    size = sum(2 * out.size * out.dtype.itemsize for out in outs)
    out_specs = [IN_HBM] + [VMEM] * (len(outs) - 1)
    return pl.pallas_call(
        kernel,
        out_shape=out_shape,
        in_specs=in_specs,
        out_specs=out_specs if isinstance(out_shape, list) else IN_HBM,
        input_output_aliases=aliases or {},
        scratch_shapes=scratch,
        compiler_params=pltpu.CompilerParams(vmem_limit_bytes=room),
        cost_estimate=pl.CostEstimate(flops=0, bytes_accessed=size, transcendentals=0),
    )


def home_places(late):
    for owner in range(SECTIONS):
        micro, head, half = owner // RING, owner % RING // 2, owner % 2
        block = 3 - half if late else half
        yield owner, (micro, pl.ds(block * BLOCK, BLOCK), pl.ds(head * WIDE, WIDE))


def own_units(me, raw, across):
    def kernel(me_ref, raw_ref, across_ref, *rest):
        out_refs, (held, in_sems, out_sems) = rest[:KV_HEADS], rest[KV_HEADS:]

        def take(source):
            copies = []
            for head in range(KV_HEADS):
                for part in range(2):
                    column = part * KEY_WIDTH + head * HEAD
                    slot = held.at[head, part]
                    copies.append((
                        pltpu.make_async_copy(
                            source.at[:, pl.ds(column, HEAD)], slot, in_sems.at[head, part]
                        ),
                        [pltpu.make_async_copy(
                            slot, out_refs[head].at[:, pl.ds(part * HEAD, HEAD)],
                            out_sems.at[head, part],
                        )],
                    ))
            run_copies(copies)

        pl.when(me_ref[0] < RING)(lambda: take(raw_ref.at[0]))
        pl.when(me_ref[0] >= RING)(lambda: take(across_ref))

    return pl.pallas_call(
        kernel,
        out_shape=[jax.ShapeDtypeStruct((LENGTH, 2 * HEAD), raw.dtype)] * KV_HEADS,
        in_specs=[SMEM, IN_HBM, IN_HBM],
        out_specs=[IN_HBM] * KV_HEADS,
        scratch_shapes=[
            pltpu.VMEM((KV_HEADS, 2, LENGTH, HEAD), raw.dtype),
            pltpu.SemaphoreType.DMA((KV_HEADS, 2)),
            pltpu.SemaphoreType.DMA((KV_HEADS, 2)),
        ],
        compiler_params=pltpu.CompilerParams(vmem_limit_bytes=SOME_ROOM),
        cost_estimate=pl.CostEstimate(
            flops=UNITS_FLOPS, bytes_accessed=1024 * 1024, transcendentals=0
        ),
    )(me.reshape(1), raw, across)


def pick(me, at_even, at_odd):
    def kernel(me_ref, even_ref, odd_ref, out_ref):
        out_ref[...] = jnp.where(lax.rem(me_ref[0], 2) == 0, even_ref[...], odd_ref[...])

    return pl.pallas_call(
        kernel,
        out_shape=jax.ShapeDtypeStruct(at_even.shape, at_even.dtype),
        in_specs=[SMEM, VMEM, VMEM],
        out_specs=VMEM,
        compiler_params=pltpu.CompilerParams(vmem_limit_bytes=SOME_ROOM),
        cost_estimate=pl.CostEstimate(
            flops=UNITS_FLOPS, bytes_accessed=1024 * 1024, transcendentals=0
        ),
    )(me.reshape(1), at_even, at_odd)


def cache_whole(me, *pieces):
    def kernel(me_ref, *refs):
        sources, (whole_ref, held, in_sems, out_sems) = refs[: len(GATHERED)], refs[len(GATHERED) :]
        here = me_ref[0]
        copies = []
        n = 0
        for source, places in zip(sources, GATHERED):
            later = []
            first_slot = n
            for i, back in enumerate(places):
                for side in range(2):
                    owner = lax.rem(here + RING - back, RING)
                    micro = lax.rem(here // RING + side, 2)
                    head, half = owner // 2, lax.rem(owner, 2)
                    start = pl.multiple_of(half * (LENGTH // 2), LENGTH // 2)
                    for part in range(2):
                        column = pl.multiple_of(head * HEAD + part * KEY_WIDTH, HEAD)
                        later.append(
                            pltpu.make_async_copy(
                                held.at[n, :, pl.ds(part * HEAD, HEAD)],
                                whole_ref.at[micro, pl.ds(start, LENGTH // 2), pl.ds(column, HEAD)],
                                out_sems.at[n, part],
                            )
                        )
                    n += 1
            slots = held.at[pl.ds(first_slot, n - first_slot)]
            copies.append((pltpu.make_async_copy(source, slots, in_sems.at[first_slot]), later))
        run_copies(copies)

    out = jax.ShapeDtypeStruct((MICROS, LENGTH, 2 * KEY_WIDTH), pieces[0].dtype)
    scratch = [
        pltpu.VMEM((SECTIONS, LENGTH // 2, 2 * HEAD), out.dtype),
        pltpu.SemaphoreType.DMA((SECTIONS,)),
        pltpu.SemaphoreType.DMA((SECTIONS, 2)),
    ]
    in_specs = [SMEM] + [IN_HBM] * len(pieces)
    return moving_call(kernel, out, scratch, in_specs)(me.reshape(1), *pieces)


def three_parts(rows):
    parts = []
    for i in range(GROUP):
        left = rows[i : i + 1]
        for _ in range(3):
            part = left.astype(jnp.bfloat16).astype(jnp.float32)
            parts.append(part)
            left = left - part
    parts.append(jnp.zeros_like(parts[0]))
    return jnp.concatenate(parts, axis=0).astype(jnp.bfloat16)


def from_parts(parts):
    parts = parts.astype(jnp.float32)
    return jnp.concatenate(
        [
            parts[3 * i : 3 * i + 1] + parts[3 * i + 1 : 3 * i + 2] + parts[3 * i + 2 : 3 * i + 3]
            for i in range(GROUP)
        ],
        axis=0,
    )


def pack(whole, late, gains=None):
    tall = STACK if gains is None else STACK + TAIL

    def kernel(*refs):
        whole_ref, (out_ref, held, stacked, in_sems, out_sems) = refs[-6], refs[-5:]
        arriving = [
            pltpu.make_async_copy(whole_ref.at[place], held.at[owner], in_sems.at[owner])
            for owner, place in home_places(late)
        ]
        for copy in arriving:
            copy.start()
        leaving = []
        for owner in range(SECTIONS):
            if gains is not None:
                first = owner % RING // 2 * WIDE
                heads = [refs[0][:, first + h * HEAD : first + (h + 1) * HEAD] for h in range(GROUP)]
                stacked[owner, STACK:] = three_parts(jnp.concatenate(heads, axis=0))
            arriving[owner].wait()
            for h in range(GROUP):
                stacked[owner, h * BLOCK : (h + 1) * BLOCK] = held[owner, :, h * HEAD : (h + 1) * HEAD]
            copy = pltpu.make_async_copy(stacked.at[owner], out_ref.at[owner], out_sems.at[owner])
            copy.start()
            leaving.append(copy)
        for copy in leaving:
            copy.wait()

    out = jax.ShapeDtypeStruct((SECTIONS, tall, HEAD), whole.dtype)
    scratch = [
        pltpu.VMEM((SECTIONS, BLOCK, WIDE), whole.dtype),
        pltpu.VMEM(out.shape, whole.dtype),
        pltpu.SemaphoreType.DMA((SECTIONS,)),
        pltpu.SemaphoreType.DMA((SECTIONS,)),
    ]
    if gains is None:
        return moving_call(kernel, out, scratch, [IN_HBM], room=ALL_ROOM)(whole)
    return moving_call(kernel, out, scratch, [VMEM, IN_HBM], room=ALL_ROOM)(gains, whole)


def unpack(came, late, whole=None):
    tall = came.shape[1]

    def kernel(came_ref, *rest):
        if whole is None:
            out_ref, (held, spread, in_sems, out_sems) = rest[0], rest[1:]
        else:
            _, out_ref, gain_ref, held, spread, in_sems, out_sems = rest
        arriving = [
            pltpu.make_async_copy(came_ref.at[owner], held.at[owner], in_sems.at[owner])
            for owner in range(SECTIONS)
        ]
        for copy in arriving:
            copy.start()
        leaving = []
        for owner, place in home_places(late):
            arriving[owner].wait()
            for h in range(GROUP):
                spread[owner, :, h * HEAD : (h + 1) * HEAD] = held[owner, h * BLOCK : (h + 1) * BLOCK]
            copy = pltpu.make_async_copy(spread.at[owner], out_ref.at[place], out_sems.at[owner])
            copy.start()
            leaving.append(copy)
        if whole is not None:
            for head in range(KV_HEADS):
                total = jnp.zeros((GROUP, HEAD), jnp.float32)
                for owner in (2 * head, 2 * head + 1, RING + 2 * head, RING + 2 * head + 1):
                    total += from_parts(held[owner, STACK:])
                for h in range(GROUP):
                    first = head * WIDE + h * HEAD
                    gain_ref[:, first : first + HEAD] = total[h : h + 1]
        for copy in leaving:
            copy.wait()

    out = jax.ShapeDtypeStruct((MICROS, LENGTH, HEADS * HEAD), came.dtype)
    scratch = [
        pltpu.VMEM(came.shape, came.dtype),
        pltpu.VMEM((SECTIONS, BLOCK, WIDE), came.dtype),
        pltpu.SemaphoreType.DMA((SECTIONS,)),
        pltpu.SemaphoreType.DMA((SECTIONS,)),
    ]
    if whole is None:
        return moving_call(kernel, out, scratch, [IN_HBM])(came)
    outs = [out, jax.ShapeDtypeStruct((1, HEADS * HEAD), jnp.float32)]
    return moving_call(kernel, outs, scratch, [IN_HBM, IN_HBM], {1: 0})(came, whole)


def with_gains(grads, gain_part):
    def kernel(gain_ref, _, out_ref, tails, sems):
        copies = []
        for s in range(SECTIONS):
            tails[s] = three_parts(gain_ref[s])
            copy = pltpu.make_async_copy(tails.at[s], out_ref.at[s, pl.ds(STACK, TAIL)], sems.at[s])
            copy.start()
            copies.append(copy)
        for copy in copies:
            copy.wait()

    out = jax.ShapeDtypeStruct(grads.shape, grads.dtype)
    scratch = [
        pltpu.VMEM((SECTIONS, TAIL, HEAD), grads.dtype),
        pltpu.SemaphoreType.DMA((SECTIONS,)),
    ]
    return moving_call(kernel, out, scratch, [VMEM, IN_HBM], {1: 0})(gain_part, grads)


def per_row(gains):
    return jnp.concatenate(
        [jnp.broadcast_to(gains[h : h + 1], (BLOCK, HEAD)) for h in range(GROUP)], axis=0
    )


def per_head(rows):
    sums = [
        jnp.sum(rows[h * BLOCK : (h + 1) * BLOCK], axis=0, keepdims=True) for h in range(GROUP)
    ]
    return jnp.concatenate(sums + [jnp.zeros((8 - GROUP, HEAD), jnp.float32)], axis=0)


def run_layers(saved_ref, gain_of, kv_ref, bias_ref, top_ref, grads_ref, cache_ref, add_gain):
    seen = bias_ref.shape[0]
    contract_last = (((1,), (1,)), ((), ()))
    contract_first = (((0,), (0,)), ((), ()))

    def layer(step, incoming):
        s = SECTIONS - 1 - step
        keys, values = kv_ref[:seen, :HEAD], kv_ref[:seen, HEAD:]
        gain = per_row(gain_of(s))
        saved = saved_ref[s, :STACK].astype(jnp.float32)
        queries = (saved * gain).astype(jnp.bfloat16)
        scores = lax.dot_general(keys, queries, contract_last, preferred_element_type=jnp.float32)
        scores = scores * (SCALE * LOG2E) + bias_ref[...]
        exp_terms = jnp.exp2(scores - jnp.max(scores, axis=0, keepdims=True))
        probs = exp_terms * (1.0 / jnp.sum(exp_terms, axis=0, keepdims=True))
        dprob = lax.dot_general(values, incoming, contract_last, preferred_element_type=jnp.float32)
        delta = jnp.sum(probs * dprob, axis=0, keepdims=True)
        dscore = (probs * (dprob - delta)).astype(jnp.bfloat16)
        dquery = SCALE * lax.dot_general(
            dscore, keys, contract_first, preferred_element_type=jnp.float32
        )
        cache_ref[:seen, :HEAD] += SCALE * jnp.dot(dscore, queries, preferred_element_type=jnp.float32)
        cache_ref[:seen, HEAD:] += jnp.dot(
            probs.astype(jnp.bfloat16), incoming, preferred_element_type=jnp.float32
        )
        add_gain(s, per_head(dquery * saved))
        grads = (incoming.astype(jnp.float32) + gain * dquery).astype(jnp.bfloat16)
        grads_ref[s, :STACK] = grads
        return grads

    top = jnp.concatenate([top_ref[:, h * HEAD : (h + 1) * HEAD] for h in range(GROUP)], axis=0)
    lax.fori_loop(0, SECTIONS, layer, top, unroll=2)


def late_kernel(saved_ref, kv_ref, bias_ref, top_ref, grads_ref, cache_ref, gain_ref, part_ref):
    for s in range(SECTIONS):
        gain_ref[s, :GROUP] = from_parts(saved_ref[s, STACK:])
    cache_ref[...] = jnp.zeros_like(cache_ref)

    def add_gain(s, part):
        part_ref[s] = part

    run_layers(
        saved_ref, lambda s: gain_ref[s], kv_ref, bias_ref, top_ref, grads_ref, cache_ref, add_gain
    )


def early_kernel(saved_ref, kv_ref, bias_ref, top_ref, cache_before, gain_ref, part_before,
                 grads_ref, cache_ref, part_ref):
    cache_ref[...] = cache_before[...]

    def add_gain(s, part):
        part_ref[s] = part_before[s] + part

    run_layers(
        saved_ref, lambda s: gain_ref[s], kv_ref, bias_ref, top_ref, grads_ref, cache_ref, add_gain
    )


def chain(kernel, saved, kv_unit, bias, top, grads_tall, *before):
    seen, columns = bias.shape
    shapes = [
        ((SECTIONS, grads_tall, HEAD), jnp.bfloat16),
        ((LENGTH, 2 * HEAD), jnp.float32),
        ((SECTIONS, 8, HEAD), jnp.float32),
    ]
    if not before:
        shapes.append(shapes[-1])
    return pl.pallas_call(
        kernel,
        out_shape=[jax.ShapeDtypeStruct(*shape) for shape in shapes],
        in_specs=[VMEM] * (4 + len(before)),
        out_specs=[VMEM] * len(shapes),
        compiler_params=pltpu.CompilerParams(vmem_limit_bytes=24 * 1024 * 1024),
        cost_estimate=pl.CostEstimate(
            flops=SECTIONS * 10 * columns * seen * HEAD,
            bytes_accessed=6 * 1024 * 1024,
            transcendentals=SECTIONS * columns * seen,
        ),
    )(saved, kv_unit, bias, top, *before)


def bias_of(segments, block, keys_seen):
    rows = jnp.tile(lax.dynamic_slice(segments, (block * BLOCK,), (BLOCK,)), GROUP)
    query_pos = block * BLOCK + jnp.tile(jnp.arange(BLOCK), GROUP)
    key_pos = jnp.arange(keys_seen)
    allowed = (key_pos[:, None] <= query_pos[None, :]) & (
        segments[:keys_seen, None] == rows[None, :]
    )
    return jnp.where(allowed, 0.0, MASKED).astype(jnp.float32)


def on_device(saved_inputs, query_gains, cache_slots, segment_ids, output_grad):
    me = lax.axis_index("section")
    micro, head, half = me // RING, me % RING // 2, me % 2

    segments = lax.dynamic_index_in_dim(segment_ids, micro, 0, keepdims=False)
    late_block, early_block = 3 - half, half

    def top_of(block):
        start = (micro, block * BLOCK, head * WIDE)
        return lax.dynamic_slice(output_grad, start, (1, BLOCK, WIDE))[0]

    late_bias = bias_of(segments, late_block, LENGTH)
    early_bias = bias_of(segments, early_block, LENGTH // 2)
    late_top, early_top = top_of(late_block), top_of(early_block)

    raw = cache_slots[0]
    across = moved(raw[1], [(0, RING)])
    late_saved = exchange(pack(saved_inputs[0], True, query_gains))
    ready = after(saved_inputs[0], late_bias, early_bias, late_top, early_top)
    early_packed = pack(ready, False)
    four = own_units(me, raw, after(across, early_packed))
    came = [moved(four[k], [(0, 2 * k), (RING, RING + 2 * k)]) for k in (2, 1, 3)]
    at_even = jnp.where(me % RING == 0, four[0], came[0] + came[1] + came[2])
    at_even = after(at_even, early_packed)
    at_odd = moved(at_even, [(i, i + 1) for i in range(0, SECTIONS, 2)])
    kv_unit = pick(me, at_even, at_odd)
    early_saved = exchange(after(early_packed, late_saved, at_even))

    late_grads, cache_part, gains, gain_part = chain(
        late_kernel, late_saved, kv_unit, late_bias, late_top, STACK,
    )
    late_home = exchange(late_grads)
    early_grads, cache_part, gain_part = chain(
        early_kernel, early_saved, kv_unit, early_bias, early_top, STACK + TAIL,
        cache_part, gains, gain_part,
    )
    halves = cache_part.reshape(2, LENGTH // 2, 2 * HEAD)
    theirs = swapped(lax.dynamic_index_in_dim(halves, 1 - half, 0, keepdims=False), 1)
    for bit in (1, 2, 4, 8):
        gain_part = gain_part + swapped(gain_part, bit, "dp")
    early_grads = with_gains(early_grads, gain_part)

    early_home = exchange(after(early_grads, late_home, theirs))
    mine = lax.dynamic_index_in_dim(halves, half, 0, keepdims=False) + theirs
    mine = after(mine.astype(jnp.bfloat16), early_grads)
    came = [swapped(mine, bit) for bit in (4, 12, 8)]
    whole = unpack(late_home, True)
    here = jnp.stack([mine, came[2]])
    both = jnp.stack([mine, came[2], came[0], came[1]])
    both, here = lax.optimization_barrier((both, here, whole, early_home))[:2]
    pieces = [both, turned(both, 1), turned(both, -1), turned(here, 2), turned(here, -2)]
    cache_grad = cache_whole(me, *pieces)
    layer_out, gain_sum = unpack(early_home, False, whole)
    return (layer_out[None], cache_grad, gain_sum)


def solution(mesh):
    return jax.shard_map(
        on_device,
        mesh=mesh,
        in_specs=(
            P("section", "dp", None, None),
            P("section", None),
            P("section", "dp", None, None),
            P("dp", None),
            P("dp", None, None),
        ),
        out_specs=(P("section", "dp", None, None), P("dp", None, None), P("section", None)),
        check_vma=False,
    )
```

```python
import jax
import jax.numpy as jnp
from jax import lax
from jax.experimental import pallas as pl
from jax.experimental.pallas import tpu as pltpu
from jax.sharding import PartitionSpec as P

HEADS = 20
KV_HEADS = 4
HEAD = 128
GROUP = HEADS // KV_HEADS
WIDE = GROUP * HEAD
STACK = GROUP * 64
TAIL = 16
KEY_WIDTH = KV_HEADS * HEAD
SECTIONS = 16
RING = 8
MICROS = 2
LENGTH = 256
BLOCK = 64
LOG2E = 1.4426950408889634
SCALE = HEAD ** -0.5
MASKED = -1e30
RING_ORDER = (4, 3, 5, 2, 6, 1, 7)
UNITS_FLOPS = 40_000_000_000
ALL_ROOM = 56 * 1024 * 1024
SOME_ROOM = 12 * 1024 * 1024
GATHERED = ((0, 4), (1, 5), (7, 3), (2,), (6,))

VMEM = pl.BlockSpec(memory_space=pltpu.VMEM)
SMEM = pl.BlockSpec(memory_space=pltpu.SMEM)
IN_HBM = pl.BlockSpec(memory_space=pltpu.HBM)


def moved(array, pairs):
    return lax.ppermute(array, "section", pairs)


def turned(array, by):
    return moved(array, [(i, i // RING * RING + (i + by) % RING) for i in range(SECTIONS)])


def swapped(array, bit, axis="section"):
    return lax.ppermute(array, axis, [(i, i ^ bit) for i in range(16)])


def exchange(array):
    return lax.all_to_all(array, "section", 0, 0, tiled=True)


def after(array, *others):
    return lax.optimization_barrier((array, *others))[0]


def run_copies(stages):
    for first, _ in stages:
        first.start()
    for first, later in stages:
        first.wait()
        for copy in later:
            copy.start()
    for _, later in stages:
        for copy in later:
            copy.wait()


def moving_call(kernel, out_shape, scratch, in_specs, aliases=None, room=SOME_ROOM):
    outs = out_shape if isinstance(out_shape, list) else [out_shape]
    size = sum(2 * out.size * out.dtype.itemsize for out in outs)
    out_specs = [IN_HBM] + [VMEM] * (len(outs) - 1)
    return pl.pallas_call(
        kernel,
        out_shape=out_shape,
        in_specs=in_specs,
        out_specs=out_specs if isinstance(out_shape, list) else IN_HBM,
        input_output_aliases=aliases or {},
        scratch_shapes=scratch,
        compiler_params=pltpu.CompilerParams(vmem_limit_bytes=room),
        cost_estimate=pl.CostEstimate(flops=0, bytes_accessed=size, transcendentals=0),
    )


def home_places(late):
    for owner in range(SECTIONS):
        micro, head, half = owner // RING, owner % RING // 2, owner % 2
        block = 3 - half if late else half
        yield owner, (micro, pl.ds(block * BLOCK, BLOCK), pl.ds(head * WIDE, WIDE))


def own_units(me, raw, across):
    def kernel(me_ref, raw_ref, across_ref, *rest):
        out_refs, (held, in_sems, out_sems) = rest[:KV_HEADS], rest[KV_HEADS:]

        def take(source):
            copies = []
            for head in range(KV_HEADS):
                for part in range(2):
                    column = part * KEY_WIDTH + head * HEAD
                    slot = held.at[head, part]
                    copies.append((
                        pltpu.make_async_copy(
                            source.at[:, pl.ds(column, HEAD)], slot, in_sems.at[head, part]
                        ),
                        [pltpu.make_async_copy(
                            slot, out_refs[head].at[:, pl.ds(part * HEAD, HEAD)],
                            out_sems.at[head, part],
                        )],
                    ))
            run_copies(copies)

        pl.when(me_ref[0] < RING)(lambda: take(raw_ref.at[0]))
        pl.when(me_ref[0] >= RING)(lambda: take(across_ref))

    return pl.pallas_call(
        kernel,
        out_shape=[jax.ShapeDtypeStruct((LENGTH, 2 * HEAD), raw.dtype)] * KV_HEADS,
        in_specs=[SMEM, IN_HBM, IN_HBM],
        out_specs=[IN_HBM] * KV_HEADS,
        scratch_shapes=[
            pltpu.VMEM((KV_HEADS, 2, LENGTH, HEAD), raw.dtype),
            pltpu.SemaphoreType.DMA((KV_HEADS, 2)),
            pltpu.SemaphoreType.DMA((KV_HEADS, 2)),
        ],
        compiler_params=pltpu.CompilerParams(vmem_limit_bytes=SOME_ROOM),
        cost_estimate=pl.CostEstimate(
            flops=UNITS_FLOPS, bytes_accessed=1024 * 1024, transcendentals=0
        ),
    )(me.reshape(1), raw, across)


def pick(me, at_first, at_second):
    def kernel(me_ref, first_ref, second_ref, out_ref):
        z = lax.rem(me_ref[0], RING)
        first = lax.rem(z, 2) == z // 4
        out_ref[...] = jnp.where(first, first_ref[...], second_ref[...])

    return pl.pallas_call(
        kernel,
        out_shape=jax.ShapeDtypeStruct(at_first.shape, at_first.dtype),
        in_specs=[SMEM, VMEM, VMEM],
        out_specs=VMEM,
        compiler_params=pltpu.CompilerParams(vmem_limit_bytes=SOME_ROOM),
        cost_estimate=pl.CostEstimate(
            flops=UNITS_FLOPS, bytes_accessed=1024 * 1024, transcendentals=0
        ),
    )(me.reshape(1), at_first, at_second)


def cache_whole(me, *pieces):
    def kernel(me_ref, *refs):
        sources, (whole_ref, sems) = refs[: len(GATHERED)], refs[len(GATHERED) :]
        here = me_ref[0]
        copies = []
        for source, places in zip(sources, GATHERED):
            for i, back in enumerate(places):
                for side in range(2):
                    owner = lax.rem(here + RING - back, RING)
                    micro = lax.rem(here // RING + side, 2)
                    head, half = owner // 2, lax.rem(owner, 2)
                    start = pl.multiple_of(half * (LENGTH // 2), LENGTH // 2)
                    for part in range(2):
                        column = pl.multiple_of(head * HEAD + part * KEY_WIDTH, HEAD)
                        copies.append(
                            pltpu.make_async_copy(
                                source.at[2 * i + side, :, pl.ds(part * HEAD, HEAD)],
                                whole_ref.at[micro, pl.ds(start, LENGTH // 2), pl.ds(column, HEAD)],
                                sems.at[len(copies)],
                            )
                        )
        for copy in copies:
            copy.start()
        for copy in copies:
            copy.wait()

    out = jax.ShapeDtypeStruct((MICROS, LENGTH, 2 * KEY_WIDTH), pieces[0].dtype)
    scratch = [pltpu.SemaphoreType.DMA((2 * SECTIONS,))]
    in_specs = [SMEM] + [VMEM] * len(pieces)
    return moving_call(kernel, out, scratch, in_specs)(me.reshape(1), *pieces)


def three_parts(rows):
    parts = []
    for i in range(GROUP):
        left = rows[i : i + 1]
        for _ in range(3):
            part = left.astype(jnp.bfloat16).astype(jnp.float32)
            parts.append(part)
            left = left - part
    parts.append(jnp.zeros_like(parts[0]))
    return jnp.concatenate(parts, axis=0).astype(jnp.bfloat16)


def from_parts(parts):
    parts = parts.astype(jnp.float32)
    return jnp.concatenate(
        [
            parts[3 * i : 3 * i + 1] + parts[3 * i + 1 : 3 * i + 2] + parts[3 * i + 2 : 3 * i + 3]
            for i in range(GROUP)
        ],
        axis=0,
    )


def pack(whole, late, gains=None):
    tall = STACK if gains is None else STACK + TAIL

    def kernel(*refs):
        whole_ref, (out_ref, held, stacked, in_sems, out_sems) = refs[-6], refs[-5:]
        arriving = [
            pltpu.make_async_copy(whole_ref.at[place], held.at[owner], in_sems.at[owner])
            for owner, place in home_places(late)
        ]
        for copy in arriving:
            copy.start()
        if gains is not None:
            rows = [refs[0][:, i * HEAD : (i + 1) * HEAD] for i in range(HEADS)]
            parts = [
                three_parts(jnp.concatenate(rows[k * GROUP : (k + 1) * GROUP], axis=0))
                for k in range(KV_HEADS)
            ]
        leaving = []
        for owner in range(SECTIONS):
            if gains is not None:
                stacked[owner, STACK:] = parts[owner % RING // 2]
            arriving[owner].wait()
            for h in range(GROUP):
                stacked[owner, h * BLOCK : (h + 1) * BLOCK] = held[owner, :, h * HEAD : (h + 1) * HEAD]
            copy = pltpu.make_async_copy(stacked.at[owner], out_ref.at[owner], out_sems.at[owner])
            copy.start()
            leaving.append(copy)
        for copy in leaving:
            copy.wait()

    out = jax.ShapeDtypeStruct((SECTIONS, tall, HEAD), whole.dtype)
    scratch = [
        pltpu.VMEM((SECTIONS, BLOCK, WIDE), whole.dtype),
        pltpu.VMEM(out.shape, whole.dtype),
        pltpu.SemaphoreType.DMA((SECTIONS,)),
        pltpu.SemaphoreType.DMA((SECTIONS,)),
    ]
    if gains is None:
        return moving_call(kernel, out, scratch, [IN_HBM])(whole)
    return moving_call(kernel, out, scratch, [VMEM, IN_HBM], room=ALL_ROOM)(gains, whole)


def unpack(came, late, whole=None):
    def kernel(came_ref, *rest):
        if whole is None:
            out_ref, (held, spread, in_sems, out_sems) = rest[0], rest[1:]
        else:
            _, out_ref, gain_ref, spread, out_sems = rest
            held = came_ref
        if whole is None:
            arriving = [
                pltpu.make_async_copy(came_ref.at[owner], held.at[owner], in_sems.at[owner])
                for owner in range(SECTIONS)
            ]
            for copy in arriving:
                copy.start()
        leaving = []
        for owner, place in home_places(late):
            if whole is None:
                arriving[owner].wait()
            for h in range(GROUP):
                spread[owner, :, h * HEAD : (h + 1) * HEAD] = held[owner, h * BLOCK : (h + 1) * BLOCK]
            copy = pltpu.make_async_copy(spread.at[owner], out_ref.at[place], out_sems.at[owner])
            copy.start()
            leaving.append(copy)
        if whole is not None:
            for head in range(KV_HEADS):
                total = jnp.zeros((GROUP, HEAD), jnp.float32)
                for owner in (2 * head, 2 * head + 1, RING + 2 * head, RING + 2 * head + 1):
                    total += from_parts(held[owner, STACK:])
                for h in range(GROUP):
                    first = head * WIDE + h * HEAD
                    gain_ref[:, first : first + HEAD] = total[h : h + 1]
        for copy in leaving:
            copy.wait()

    out = jax.ShapeDtypeStruct((MICROS, LENGTH, HEADS * HEAD), came.dtype)
    scratch = [
        pltpu.VMEM((SECTIONS, BLOCK, WIDE), came.dtype),
        pltpu.SemaphoreType.DMA((SECTIONS,)),
    ]
    if whole is None:
        first = [pltpu.VMEM(came.shape, came.dtype), scratch[0], scratch[1], scratch[1]]
        return moving_call(kernel, out, first, [IN_HBM])(came)
    outs = [out, jax.ShapeDtypeStruct((1, HEADS * HEAD), jnp.float32)]
    return moving_call(kernel, outs, scratch, [VMEM, IN_HBM], {1: 0})(came, whole)


def with_gains(grads, gain_part):
    def kernel(gain_ref, _, out_ref, tails, sems):
        copies = []
        for s in range(SECTIONS):
            tails[s] = three_parts(gain_ref[s])
            copy = pltpu.make_async_copy(tails.at[s], out_ref.at[s, pl.ds(STACK, TAIL)], sems.at[s])
            copy.start()
            copies.append(copy)
        for copy in copies:
            copy.wait()

    out = jax.ShapeDtypeStruct(grads.shape, grads.dtype)
    scratch = [
        pltpu.VMEM((SECTIONS, TAIL, HEAD), grads.dtype),
        pltpu.SemaphoreType.DMA((SECTIONS,)),
    ]
    return moving_call(kernel, out, scratch, [VMEM, IN_HBM], {1: 0})(gain_part, grads)


def per_row(gains):
    return jnp.concatenate(
        [jnp.broadcast_to(gains[h : h + 1], (BLOCK, HEAD)) for h in range(GROUP)], axis=0
    )


def per_head(rows):
    sums = [
        jnp.sum(rows[h * BLOCK : (h + 1) * BLOCK], axis=0, keepdims=True) for h in range(GROUP)
    ]
    return jnp.concatenate(sums + [jnp.zeros((8 - GROUP, HEAD), jnp.float32)], axis=0)


def run_layers(saved_ref, gain_of, kv_ref, bias_ref, top_ref, grads_ref, cache_ref, add_gain):
    seen = bias_ref.shape[0]
    contract_last = (((1,), (1,)), ((), ()))
    contract_first = (((0,), (0,)), ((), ()))

    def layer(step, incoming):
        s = SECTIONS - 1 - step
        keys, values = kv_ref[:seen, :HEAD], kv_ref[:seen, HEAD:]
        gain = per_row(gain_of(s))
        saved = saved_ref[s, :STACK].astype(jnp.float32)
        queries = (saved * gain).astype(jnp.bfloat16)
        scores = lax.dot_general(keys, queries, contract_last, preferred_element_type=jnp.float32)
        scores = scores * (SCALE * LOG2E) + bias_ref[...]
        exp_terms = jnp.exp2(scores - jnp.max(scores, axis=0, keepdims=True))
        probs = exp_terms * (1.0 / jnp.sum(exp_terms, axis=0, keepdims=True))
        dprob = lax.dot_general(values, incoming, contract_last, preferred_element_type=jnp.float32)
        delta = jnp.sum(probs * dprob, axis=0, keepdims=True)
        dscore = (probs * (dprob - delta)).astype(jnp.bfloat16)
        dquery = SCALE * lax.dot_general(
            dscore, keys, contract_first, preferred_element_type=jnp.float32
        )
        cache_ref[:seen, :HEAD] += SCALE * jnp.dot(dscore, queries, preferred_element_type=jnp.float32)
        cache_ref[:seen, HEAD:] += jnp.dot(
            probs.astype(jnp.bfloat16), incoming, preferred_element_type=jnp.float32
        )
        add_gain(s, per_head(dquery * saved))
        grads = (incoming.astype(jnp.float32) + gain * dquery).astype(jnp.bfloat16)
        grads_ref[s, :STACK] = grads
        return grads

    top = jnp.concatenate([top_ref[:, h * HEAD : (h + 1) * HEAD] for h in range(GROUP)], axis=0)
    lax.fori_loop(0, SECTIONS, layer, top, unroll=2)


def late_kernel(saved_ref, kv_ref, bias_ref, top_ref, grads_ref, cache_ref, gain_ref, part_ref):
    for s in range(SECTIONS):
        gain_ref[s, :GROUP] = from_parts(saved_ref[s, STACK:])
    cache_ref[...] = jnp.zeros_like(cache_ref)

    def add_gain(s, part):
        part_ref[s] = part

    run_layers(
        saved_ref, lambda s: gain_ref[s], kv_ref, bias_ref, top_ref, grads_ref, cache_ref, add_gain
    )


def early_kernel(saved_ref, kv_ref, bias_ref, top_ref, cache_before, gain_ref, part_before,
                 grads_ref, cache_ref, part_ref):
    cache_ref[...] = cache_before[...]

    def add_gain(s, part):
        part_ref[s] = part_before[s] + part

    run_layers(
        saved_ref, lambda s: gain_ref[s], kv_ref, bias_ref, top_ref, grads_ref, cache_ref, add_gain
    )


def chain(kernel, saved, kv_unit, bias, top, grads_tall, *before):
    seen, columns = bias.shape
    shapes = [
        ((SECTIONS, grads_tall, HEAD), jnp.bfloat16),
        ((LENGTH, 2 * HEAD), jnp.float32),
        ((SECTIONS, 8, HEAD), jnp.float32),
    ]
    if not before:
        shapes.append(shapes[-1])
    return pl.pallas_call(
        kernel,
        out_shape=[jax.ShapeDtypeStruct(*shape) for shape in shapes],
        in_specs=[VMEM] * (4 + len(before)),
        out_specs=[VMEM] * len(shapes),
        compiler_params=pltpu.CompilerParams(vmem_limit_bytes=24 * 1024 * 1024),
        cost_estimate=pl.CostEstimate(
            flops=SECTIONS * 10 * columns * seen * HEAD,
            bytes_accessed=6 * 1024 * 1024,
            transcendentals=SECTIONS * columns * seen,
        ),
    )(saved, kv_unit, bias, top, *before)


def bias_of(segments, block, keys_seen):
    rows = jnp.tile(lax.dynamic_slice(segments, (block * BLOCK,), (BLOCK,)), GROUP)
    query_pos = block * BLOCK + jnp.tile(jnp.arange(BLOCK), GROUP)
    key_pos = jnp.arange(keys_seen)
    allowed = (key_pos[:, None] <= query_pos[None, :]) & (
        segments[:keys_seen, None] == rows[None, :]
    )
    return jnp.where(allowed, 0.0, MASKED).astype(jnp.float32)


def on_device(saved_inputs, query_gains, cache_slots, segment_ids, output_grad):
    me = lax.axis_index("section")
    micro, head, half = me // RING, me % RING // 2, me % 2

    segments = lax.dynamic_index_in_dim(segment_ids, micro, 0, keepdims=False)
    late_block, early_block = 3 - half, half

    def top_of(block):
        start = (micro, block * BLOCK, head * WIDE)
        return lax.dynamic_slice(output_grad, start, (1, BLOCK, WIDE))[0]

    late_bias = bias_of(segments, late_block, LENGTH)
    early_bias = bias_of(segments, early_block, LENGTH // 2)
    late_top, early_top = top_of(late_block), top_of(early_block)

    raw = cache_slots[0]
    across = moved(raw[1], [(0, RING)])
    late_saved = exchange(pack(saved_inputs[0], True, query_gains))
    ready = after(saved_inputs[0], late_bias, early_bias, late_top, early_top)
    early_packed = pack(ready, False)
    four = own_units(me, raw, after(across, early_packed))
    came = [moved(four[k], [(0, z), (RING, RING + z)]) for k, z in ((2, 5), (1, 2), (3, 7))]
    at_first = jnp.where(me % RING == 0, four[0], came[0] + came[1] + came[2])
    at_first = after(at_first, early_packed)
    onward = ((0, 1), (2, 3), (5, 4), (7, 6))
    at_second = moved(at_first, [(x + i, x + j) for x in (0, RING) for i, j in onward])
    kv_unit = pick(me, at_first, at_second)
    early_saved = exchange(after(early_packed, late_saved, at_first))

    late_grads, cache_part, gains, gain_part = chain(
        late_kernel, late_saved, kv_unit, late_bias, late_top, STACK,
    )
    late_home = exchange(late_grads)
    early_grads, cache_part, gain_part = chain(
        early_kernel, early_saved, kv_unit, early_bias, early_top, STACK + TAIL,
        cache_part, gains, gain_part,
    )
    halves = cache_part.reshape(2, LENGTH // 2, 2 * HEAD)
    theirs = swapped(lax.dynamic_index_in_dim(halves, 1 - half, 0, keepdims=False), 1)
    for bit in (1, 2, 4, 8):
        gain_part = gain_part + swapped(gain_part, bit, "dp")
    early_grads = with_gains(early_grads, gain_part)

    early_home = exchange(after(early_grads, late_home, theirs))
    mine = lax.dynamic_index_in_dim(halves, half, 0, keepdims=False) + theirs
    mine = after(mine.astype(jnp.bfloat16), early_grads)
    came = [swapped(mine, bit) for bit in (4, 12, 8)]
    whole = unpack(late_home, True)
    here = jnp.stack([mine, came[2]])
    both = jnp.stack([mine, came[2], came[0], came[1]])
    both, here = lax.optimization_barrier((both, here, whole, early_home))[:2]
    pieces = [both, turned(both, 1), turned(both, -1), turned(here, 2), turned(here, -2)]
    cache_grad = cache_whole(me, *pieces)
    layer_out, gain_sum = unpack(early_home, False, whole)
    return (layer_out[None], cache_grad, gain_sum)


def solution(mesh):
    return jax.shard_map(
        on_device,
        mesh=mesh,
        in_specs=(
            P("section", "dp", None, None),
            P("section", None),
            P("section", "dp", None, None),
            P("dp", None),
            P("dp", None, None),
        ),
        out_specs=(P("section", "dp", None, None), P("dp", None, None), P("section", None)),
        check_vma=False,
    )
```

```python
import jax
import jax.numpy as jnp
from jax import lax
from jax.experimental import pallas as pl
from jax.experimental.pallas import tpu as pltpu
from jax.sharding import PartitionSpec as P

HEADS = 20
KV_HEADS = 4
HEAD = 128
GROUP = HEADS // KV_HEADS
WIDE = GROUP * HEAD
STACK = GROUP * 64
TAIL = 16
KEY_WIDTH = KV_HEADS * HEAD
SECTIONS = 16
RING = 8
MICROS = 2
LENGTH = 256
BLOCK = 64
LOG2E = 1.4426950408889634
SCALE = HEAD ** -0.5
MASKED = -1e30
RING_ORDER = (4, 3, 5, 2, 6, 1, 7)
UNITS_FLOPS = 40_000_000_000
ALL_ROOM = 56 * 1024 * 1024
SOME_ROOM = 12 * 1024 * 1024
GATHERED = ((0, 4), (1, 5), (7, 3), (2, 6))

VMEM = pl.BlockSpec(memory_space=pltpu.VMEM)
SMEM = pl.BlockSpec(memory_space=pltpu.SMEM)
IN_HBM = pl.BlockSpec(memory_space=pltpu.HBM)


def moved(array, pairs):
    return lax.ppermute(array, "section", pairs)


def turned(array, by):
    return moved(array, [(i, i // RING * RING + (i + by) % RING) for i in range(SECTIONS)])


def swapped(array, bit, axis="section"):
    return lax.ppermute(array, axis, [(i, i ^ bit) for i in range(16)])


def exchange(array):
    return lax.all_to_all(array, "section", 0, 0, tiled=True)


def after(array, *others):
    return lax.optimization_barrier((array, *others))[0]


def run_copies(stages):
    for first, _ in stages:
        first.start()
    for first, later in stages:
        first.wait()
        for copy in later:
            copy.start()
    for _, later in stages:
        for copy in later:
            copy.wait()


def moving_call(kernel, out_shape, scratch, in_specs, aliases=None, room=SOME_ROOM):
    outs = out_shape if isinstance(out_shape, list) else [out_shape]
    size = sum(2 * out.size * out.dtype.itemsize for out in outs)
    out_specs = [IN_HBM] + [VMEM] * (len(outs) - 1)
    return pl.pallas_call(
        kernel,
        out_shape=out_shape,
        in_specs=in_specs,
        out_specs=out_specs if isinstance(out_shape, list) else IN_HBM,
        input_output_aliases=aliases or {},
        scratch_shapes=scratch,
        compiler_params=pltpu.CompilerParams(vmem_limit_bytes=room),
        cost_estimate=pl.CostEstimate(flops=0, bytes_accessed=size, transcendentals=0),
    )


def home_places(late):
    for owner in range(SECTIONS):
        micro, head, half = owner // RING, owner % RING // 2, owner % 2
        block = 3 - half if late else half
        yield owner, (micro, pl.ds(block * BLOCK, BLOCK), pl.ds(head * WIDE, WIDE))


def own_units(me, raw, across):
    def kernel(me_ref, raw_ref, across_ref, *rest):
        out_refs, (held, in_sems, out_sems) = rest[:KV_HEADS], rest[KV_HEADS:]

        def take(source):
            copies = []
            for head in range(KV_HEADS):
                for part in range(2):
                    column = part * KEY_WIDTH + head * HEAD
                    slot = held.at[head, part]
                    copies.append((
                        pltpu.make_async_copy(
                            source.at[:, pl.ds(column, HEAD)], slot, in_sems.at[head, part]
                        ),
                        [pltpu.make_async_copy(
                            slot, out_refs[head].at[:, pl.ds(part * HEAD, HEAD)],
                            out_sems.at[head, part],
                        )],
                    ))
            run_copies(copies)

        pl.when(me_ref[0] < RING)(lambda: take(raw_ref.at[0]))
        pl.when(me_ref[0] >= RING)(lambda: take(across_ref))

    return pl.pallas_call(
        kernel,
        out_shape=[jax.ShapeDtypeStruct((LENGTH, 2 * HEAD), raw.dtype)] * KV_HEADS,
        in_specs=[SMEM, IN_HBM, IN_HBM],
        out_specs=[IN_HBM] * KV_HEADS,
        scratch_shapes=[
            pltpu.VMEM((KV_HEADS, 2, LENGTH, HEAD), raw.dtype),
            pltpu.SemaphoreType.DMA((KV_HEADS, 2)),
            pltpu.SemaphoreType.DMA((KV_HEADS, 2)),
        ],
        compiler_params=pltpu.CompilerParams(vmem_limit_bytes=SOME_ROOM),
        cost_estimate=pl.CostEstimate(
            flops=UNITS_FLOPS, bytes_accessed=1024 * 1024, transcendentals=0
        ),
    )(me.reshape(1), raw, across)


def pick(me, at_first, at_second):
    def kernel(me_ref, first_ref, second_ref, out_ref):
        z = lax.rem(me_ref[0], RING)
        first = lax.rem(z, 2) == z // 4
        out_ref[...] = jnp.where(first, first_ref[...], second_ref[...])

    return pl.pallas_call(
        kernel,
        out_shape=jax.ShapeDtypeStruct(at_first.shape, at_first.dtype),
        in_specs=[SMEM, VMEM, VMEM],
        out_specs=VMEM,
        compiler_params=pltpu.CompilerParams(vmem_limit_bytes=SOME_ROOM),
        cost_estimate=pl.CostEstimate(
            flops=UNITS_FLOPS, bytes_accessed=1024 * 1024, transcendentals=0
        ),
    )(me.reshape(1), at_first, at_second)


def cache_whole(me, *pieces):
    def kernel(me_ref, *refs):
        sources, (whole_ref, sems) = refs[: len(GATHERED)], refs[len(GATHERED) :]
        here = me_ref[0]
        copies = []
        for n, (source, places) in enumerate(zip(sources, GATHERED)):
            for i, back in enumerate(places):
                if n == len(GATHERED) - 1:
                    back = back + (1 - 2 * i) * 4 * lax.rem(here, 2)
                for side in range(2):
                    owner = lax.rem(here + RING - back, RING)
                    micro = lax.rem(here // RING + side, 2)
                    head, half = owner // 2, lax.rem(owner, 2)
                    start = pl.multiple_of(half * (LENGTH // 2), LENGTH // 2)
                    for part in range(2):
                        column = pl.multiple_of(head * HEAD + part * KEY_WIDTH, HEAD)
                        copies.append(
                            pltpu.make_async_copy(
                                source.at[2 * i + side, :, pl.ds(part * HEAD, HEAD)],
                                whole_ref.at[micro, pl.ds(start, LENGTH // 2), pl.ds(column, HEAD)],
                                sems.at[len(copies)],
                            )
                        )
        for copy in copies:
            copy.start()
        for copy in copies:
            copy.wait()

    out = jax.ShapeDtypeStruct((MICROS, LENGTH, 2 * KEY_WIDTH), pieces[0].dtype)
    scratch = [pltpu.SemaphoreType.DMA((2 * SECTIONS,))]
    in_specs = [SMEM] + [VMEM] * len(pieces)
    return moving_call(kernel, out, scratch, in_specs)(me.reshape(1), *pieces)


def three_parts(rows):
    parts = []
    for i in range(GROUP):
        left = rows[i : i + 1]
        for _ in range(3):
            part = left.astype(jnp.bfloat16).astype(jnp.float32)
            parts.append(part)
            left = left - part
    parts.append(jnp.zeros_like(parts[0]))
    return jnp.concatenate(parts, axis=0).astype(jnp.bfloat16)


def from_parts(parts):
    parts = parts.astype(jnp.float32)
    return jnp.concatenate(
        [
            parts[3 * i : 3 * i + 1] + parts[3 * i + 1 : 3 * i + 2] + parts[3 * i + 2 : 3 * i + 3]
            for i in range(GROUP)
        ],
        axis=0,
    )


def pack(whole, late, gains=None):
    tall = STACK if gains is None else STACK + TAIL

    def kernel(*refs):
        whole_ref, (out_ref, held, stacked, in_sems, out_sems) = refs[-6], refs[-5:]
        arriving = [
            pltpu.make_async_copy(whole_ref.at[place], held.at[owner], in_sems.at[owner])
            for owner, place in home_places(late)
        ]
        for copy in arriving:
            copy.start()
        if gains is not None:
            rows = [refs[0][:, i * HEAD : (i + 1) * HEAD] for i in range(HEADS)]
            parts = [
                three_parts(jnp.concatenate(rows[k * GROUP : (k + 1) * GROUP], axis=0))
                for k in range(KV_HEADS)
            ]
        leaving = []
        for owner in range(SECTIONS):
            if gains is not None:
                stacked[owner, STACK:] = parts[owner % RING // 2]
            arriving[owner].wait()
            for h in range(GROUP):
                stacked[owner, h * BLOCK : (h + 1) * BLOCK] = held[owner, :, h * HEAD : (h + 1) * HEAD]
            copy = pltpu.make_async_copy(stacked.at[owner], out_ref.at[owner], out_sems.at[owner])
            copy.start()
            leaving.append(copy)
        for copy in leaving:
            copy.wait()

    out = jax.ShapeDtypeStruct((SECTIONS, tall, HEAD), whole.dtype)
    scratch = [
        pltpu.VMEM((SECTIONS, BLOCK, WIDE), whole.dtype),
        pltpu.VMEM(out.shape, whole.dtype),
        pltpu.SemaphoreType.DMA((SECTIONS,)),
        pltpu.SemaphoreType.DMA((SECTIONS,)),
    ]
    if gains is None:
        return moving_call(kernel, out, scratch, [IN_HBM])(whole)
    return moving_call(kernel, out, scratch, [VMEM, IN_HBM], room=ALL_ROOM)(gains, whole)


def unpack(came, late, whole=None):
    def kernel(came_ref, *rest):
        if whole is None:
            out_ref, (held, spread, in_sems, out_sems) = rest[0], rest[1:]
        else:
            _, out_ref, gain_ref, spread, out_sems = rest
            held = came_ref
        if whole is None:
            arriving = [
                pltpu.make_async_copy(came_ref.at[owner], held.at[owner], in_sems.at[owner])
                for owner in range(SECTIONS)
            ]
            for copy in arriving:
                copy.start()
        leaving = []
        for owner, place in home_places(late):
            if whole is None:
                arriving[owner].wait()
            for h in range(GROUP):
                spread[owner, :, h * HEAD : (h + 1) * HEAD] = held[owner, h * BLOCK : (h + 1) * BLOCK]
            copy = pltpu.make_async_copy(spread.at[owner], out_ref.at[place], out_sems.at[owner])
            copy.start()
            leaving.append(copy)
        if whole is not None:
            for head in range(KV_HEADS):
                total = jnp.zeros((GROUP, HEAD), jnp.float32)
                for owner in (2 * head, 2 * head + 1, RING + 2 * head, RING + 2 * head + 1):
                    total += from_parts(held[owner, STACK:])
                for h in range(GROUP):
                    first = head * WIDE + h * HEAD
                    gain_ref[:, first : first + HEAD] = total[h : h + 1]
        for copy in leaving:
            copy.wait()

    out = jax.ShapeDtypeStruct((MICROS, LENGTH, HEADS * HEAD), came.dtype)
    scratch = [
        pltpu.VMEM((SECTIONS, BLOCK, WIDE), came.dtype),
        pltpu.SemaphoreType.DMA((SECTIONS,)),
    ]
    if whole is None:
        first = [pltpu.VMEM(came.shape, came.dtype), scratch[0], scratch[1], scratch[1]]
        return moving_call(kernel, out, first, [IN_HBM])(came)
    outs = [out, jax.ShapeDtypeStruct((1, HEADS * HEAD), jnp.float32)]
    return moving_call(kernel, outs, scratch, [VMEM, IN_HBM], {1: 0})(came, whole)


def with_gains(grads, gain_part):
    def kernel(gain_ref, _, out_ref, tails, sems):
        copies = []
        for s in range(SECTIONS):
            tails[s] = three_parts(gain_ref[s])
            copy = pltpu.make_async_copy(tails.at[s], out_ref.at[s, pl.ds(STACK, TAIL)], sems.at[s])
            copy.start()
            copies.append(copy)
        for copy in copies:
            copy.wait()

    out = jax.ShapeDtypeStruct(grads.shape, grads.dtype)
    scratch = [
        pltpu.VMEM((SECTIONS, TAIL, HEAD), grads.dtype),
        pltpu.SemaphoreType.DMA((SECTIONS,)),
    ]
    return moving_call(kernel, out, scratch, [VMEM, IN_HBM], {1: 0})(gain_part, grads)


def per_row(gains):
    return jnp.concatenate(
        [jnp.broadcast_to(gains[h : h + 1], (BLOCK, HEAD)) for h in range(GROUP)], axis=0
    )


def per_head(rows):
    sums = [
        jnp.sum(rows[h * BLOCK : (h + 1) * BLOCK], axis=0, keepdims=True) for h in range(GROUP)
    ]
    return jnp.concatenate(sums + [jnp.zeros((8 - GROUP, HEAD), jnp.float32)], axis=0)


def run_layers(saved_ref, gain_of, kv_ref, bias_ref, top_ref, grads_ref, cache_ref, add_gain):
    seen = bias_ref.shape[0]
    contract_last = (((1,), (1,)), ((), ()))
    contract_first = (((0,), (0,)), ((), ()))

    def layer(step, incoming):
        s = SECTIONS - 1 - step
        keys, values = kv_ref[:seen, :HEAD], kv_ref[:seen, HEAD:]
        gain = per_row(gain_of(s))
        saved = saved_ref[s, :STACK].astype(jnp.float32)
        queries = (saved * gain).astype(jnp.bfloat16)
        scores = lax.dot_general(keys, queries, contract_last, preferred_element_type=jnp.float32)
        scores = scores * (SCALE * LOG2E) + bias_ref[...]
        exp_terms = jnp.exp2(scores - jnp.max(scores, axis=0, keepdims=True))
        probs = exp_terms * (1.0 / jnp.sum(exp_terms, axis=0, keepdims=True))
        dprob = lax.dot_general(values, incoming, contract_last, preferred_element_type=jnp.float32)
        delta = jnp.sum(probs * dprob, axis=0, keepdims=True)
        dscore = (probs * (dprob - delta)).astype(jnp.bfloat16)
        dquery = SCALE * lax.dot_general(
            dscore, keys, contract_first, preferred_element_type=jnp.float32
        )
        cache_ref[:seen, :HEAD] += SCALE * jnp.dot(dscore, queries, preferred_element_type=jnp.float32)
        cache_ref[:seen, HEAD:] += jnp.dot(
            probs.astype(jnp.bfloat16), incoming, preferred_element_type=jnp.float32
        )
        add_gain(s, per_head(dquery * saved))
        grads = (incoming.astype(jnp.float32) + gain * dquery).astype(jnp.bfloat16)
        grads_ref[s, :STACK] = grads
        return grads

    top = jnp.concatenate([top_ref[:, h * HEAD : (h + 1) * HEAD] for h in range(GROUP)], axis=0)
    lax.fori_loop(0, SECTIONS, layer, top, unroll=2)


def late_kernel(saved_ref, kv_ref, bias_ref, top_ref, grads_ref, cache_ref, gain_ref, part_ref):
    for s in range(SECTIONS):
        gain_ref[s, :GROUP] = from_parts(saved_ref[s, STACK:])
    cache_ref[...] = jnp.zeros_like(cache_ref)

    def add_gain(s, part):
        part_ref[s] = part

    run_layers(
        saved_ref, lambda s: gain_ref[s], kv_ref, bias_ref, top_ref, grads_ref, cache_ref, add_gain
    )


def early_kernel(saved_ref, kv_ref, bias_ref, top_ref, cache_before, gain_ref, part_before,
                 grads_ref, cache_ref, part_ref):
    cache_ref[...] = cache_before[...]

    def add_gain(s, part):
        part_ref[s] = part_before[s] + part

    run_layers(
        saved_ref, lambda s: gain_ref[s], kv_ref, bias_ref, top_ref, grads_ref, cache_ref, add_gain
    )


def chain(kernel, saved, kv_unit, bias, top, grads_tall, *before):
    seen, columns = bias.shape
    shapes = [
        ((SECTIONS, grads_tall, HEAD), jnp.bfloat16),
        ((LENGTH, 2 * HEAD), jnp.float32),
        ((SECTIONS, 8, HEAD), jnp.float32),
    ]
    if not before:
        shapes.append(shapes[-1])
    return pl.pallas_call(
        kernel,
        out_shape=[jax.ShapeDtypeStruct(*shape) for shape in shapes],
        in_specs=[VMEM] * (4 + len(before)),
        out_specs=[VMEM] * len(shapes),
        compiler_params=pltpu.CompilerParams(vmem_limit_bytes=24 * 1024 * 1024),
        cost_estimate=pl.CostEstimate(
            flops=SECTIONS * 10 * columns * seen * HEAD,
            bytes_accessed=6 * 1024 * 1024,
            transcendentals=SECTIONS * columns * seen,
        ),
    )(saved, kv_unit, bias, top, *before)


def bias_of(segments, block, keys_seen):
    rows = jnp.tile(lax.dynamic_slice(segments, (block * BLOCK,), (BLOCK,)), GROUP)
    query_pos = block * BLOCK + jnp.tile(jnp.arange(BLOCK), GROUP)
    key_pos = jnp.arange(keys_seen)
    allowed = (key_pos[:, None] <= query_pos[None, :]) & (
        segments[:keys_seen, None] == rows[None, :]
    )
    return jnp.where(allowed, 0.0, MASKED).astype(jnp.float32)


def on_device(saved_inputs, query_gains, cache_slots, segment_ids, output_grad):
    me = lax.axis_index("section")
    micro, head, half = me // RING, me % RING // 2, me % 2

    segments = lax.dynamic_index_in_dim(segment_ids, micro, 0, keepdims=False)
    late_block, early_block = 3 - half, half

    def top_of(block):
        start = (micro, block * BLOCK, head * WIDE)
        return lax.dynamic_slice(output_grad, start, (1, BLOCK, WIDE))[0]

    late_bias = bias_of(segments, late_block, LENGTH)
    early_bias = bias_of(segments, early_block, LENGTH // 2)
    late_top, early_top = top_of(late_block), top_of(early_block)

    raw = cache_slots[0]
    across = moved(raw[1], [(0, RING)])
    late_saved = exchange(pack(saved_inputs[0], True, query_gains))
    ready = after(saved_inputs[0], late_bias, early_bias, late_top, early_top)
    early_packed = pack(ready, False)
    four = own_units(me, raw, after(across, early_packed))
    came = [moved(four[k], [(0, z), (RING, RING + z)]) for k, z in ((2, 5), (1, 2), (3, 7))]
    at_first = jnp.where(me % RING == 0, four[0], came[0] + came[1] + came[2])
    at_first = after(at_first, early_packed)
    onward = ((0, 1), (2, 3), (5, 4), (7, 6))
    at_second = moved(at_first, [(x + i, x + j) for x in (0, RING) for i, j in onward])
    kv_unit = pick(me, at_first, at_second)
    early_saved = exchange(after(early_packed, late_saved, at_first))

    late_grads, cache_part, gains, gain_part = chain(
        late_kernel, late_saved, kv_unit, late_bias, late_top, STACK,
    )
    late_home = exchange(late_grads)
    early_grads, cache_part, gain_part = chain(
        early_kernel, early_saved, kv_unit, early_bias, early_top, STACK + TAIL,
        cache_part, gains, gain_part,
    )
    halves = cache_part.reshape(2, LENGTH // 2, 2 * HEAD)
    theirs = lax.dynamic_index_in_dim(halves, 1 - half, 0, keepdims=False)
    theirs = swapped(theirs.astype(jnp.bfloat16), 1)
    for bit in (1, 2, 4, 8):
        gain_part = gain_part + swapped(gain_part, bit, "dp")
    early_grads = with_gains(early_grads, gain_part)

    early_home = exchange(after(early_grads, late_home, theirs))
    mine = lax.dynamic_index_in_dim(halves, half, 0, keepdims=False) + theirs
    mine = after(mine.astype(jnp.bfloat16), early_grads)
    came = [swapped(mine, bit) for bit in (4, 12, 8)]
    whole = unpack(late_home, True)
    both = jnp.stack([mine, came[2], came[0], came[1]])
    both = after(both, whole, early_home)
    inward = [(i, i // RING * RING + (i + 2 - 4 * (i % 2)) % RING) for i in range(SECTIONS)]
    pieces = [both, turned(both, 1), turned(both, -1), moved(both, inward)]
    cache_grad = cache_whole(me, *pieces)
    layer_out, gain_sum = unpack(early_home, False, whole)
    return (layer_out[None], cache_grad, gain_sum)


def solution(mesh):
    return jax.shard_map(
        on_device,
        mesh=mesh,
        in_specs=(
            P("section", "dp", None, None),
            P("section", None),
            P("section", "dp", None, None),
            P("dp", None),
            P("dp", None, None),
        ),
        out_specs=(P("section", "dp", None, None), P("dp", None, None), P("section", None)),
        check_vma=False,
    )
```

```python
import jax
import jax.numpy as jnp
from jax import lax
from jax.experimental import pallas as pl
from jax.experimental.pallas import tpu as pltpu
from jax.sharding import PartitionSpec as P

HEADS = 20
KV_HEADS = 4
HEAD = 128
GROUP = HEADS // KV_HEADS
WIDE = GROUP * HEAD
STACK = GROUP * 64
TAIL = 16
KEY_WIDTH = KV_HEADS * HEAD
SECTIONS = 16
RING = 8
MICROS = 2
LENGTH = 256
BLOCK = 64
LOG2E = 1.4426950408889634
SCALE = HEAD ** -0.5
MASKED = -1e30
RING_ORDER = (4, 3, 5, 2, 6, 1, 7)
UNITS_FLOPS = 40_000_000_000
ALL_ROOM = 56 * 1024 * 1024
SOME_ROOM = 12 * 1024 * 1024
GATHERED = ((0, 4), (1, 5), (7, 3), (2, 6))

VMEM = pl.BlockSpec(memory_space=pltpu.VMEM)
SMEM = pl.BlockSpec(memory_space=pltpu.SMEM)
IN_HBM = pl.BlockSpec(memory_space=pltpu.HBM)


def moved(array, pairs):
    return lax.ppermute(array, "section", pairs)


def turned(array, by):
    return moved(array, [(i, i // RING * RING + (i + by) % RING) for i in range(SECTIONS)])


def swapped(array, bit, axis="section"):
    return lax.ppermute(array, axis, [(i, i ^ bit) for i in range(16)])


def exchange(array):
    return lax.all_to_all(array, "section", 0, 0, tiled=True)


def after(array, *others):
    return lax.optimization_barrier((array, *others))[0]


def run_copies(stages):
    for first, _ in stages:
        first.start()
    for first, later in stages:
        first.wait()
        for copy in later:
            copy.start()
    for _, later in stages:
        for copy in later:
            copy.wait()


def moving_call(kernel, out_shape, scratch, in_specs, aliases=None, room=SOME_ROOM):
    outs = out_shape if isinstance(out_shape, list) else [out_shape]
    size = sum(2 * out.size * out.dtype.itemsize for out in outs)
    out_specs = [IN_HBM] + [VMEM] * (len(outs) - 1)
    return pl.pallas_call(
        kernel,
        out_shape=out_shape,
        in_specs=in_specs,
        out_specs=out_specs if isinstance(out_shape, list) else IN_HBM,
        input_output_aliases=aliases or {},
        scratch_shapes=scratch,
        compiler_params=pltpu.CompilerParams(vmem_limit_bytes=room),
        cost_estimate=pl.CostEstimate(flops=0, bytes_accessed=size, transcendentals=0),
    )


def home_places(late):
    for owner in range(SECTIONS):
        micro, head, half = owner // RING, owner % RING // 2, owner % 2
        block = 3 - half if late else half
        yield owner, (micro, pl.ds(block * BLOCK, BLOCK), pl.ds(head * WIDE, WIDE))


def own_units(me, raw, across):
    def kernel(me_ref, raw_ref, across_ref, *rest):
        out_refs, (held, in_sems, out_sems) = rest[:KV_HEADS], rest[KV_HEADS:]

        def take(source):
            copies = []
            for head in range(KV_HEADS):
                for part in range(2):
                    column = part * KEY_WIDTH + head * HEAD
                    slot = held.at[head, part]
                    copies.append((
                        pltpu.make_async_copy(
                            source.at[:, pl.ds(column, HEAD)], slot, in_sems.at[head, part]
                        ),
                        [pltpu.make_async_copy(
                            slot, out_refs[head].at[:, pl.ds(part * HEAD, HEAD)],
                            out_sems.at[head, part],
                        )],
                    ))
            run_copies(copies)

        pl.when(me_ref[0] < RING)(lambda: take(raw_ref.at[0]))
        pl.when(me_ref[0] >= RING)(lambda: take(across_ref))

    return pl.pallas_call(
        kernel,
        out_shape=[jax.ShapeDtypeStruct((LENGTH, 2 * HEAD), raw.dtype)] * KV_HEADS,
        in_specs=[SMEM, IN_HBM, IN_HBM],
        out_specs=[IN_HBM] * KV_HEADS,
        scratch_shapes=[
            pltpu.VMEM((KV_HEADS, 2, LENGTH, HEAD), raw.dtype),
            pltpu.SemaphoreType.DMA((KV_HEADS, 2)),
            pltpu.SemaphoreType.DMA((KV_HEADS, 2)),
        ],
        compiler_params=pltpu.CompilerParams(vmem_limit_bytes=SOME_ROOM),
        cost_estimate=pl.CostEstimate(
            flops=UNITS_FLOPS, bytes_accessed=1024 * 1024, transcendentals=0
        ),
    )(me.reshape(1), raw, across)


def pick(me, at_first, at_second):
    def kernel(me_ref, first_ref, second_ref, out_ref):
        z = lax.rem(me_ref[0], RING)
        first = lax.rem(z, 2) == z // 4
        out_ref[...] = jnp.where(first, first_ref[...], second_ref[...])

    return pl.pallas_call(
        kernel,
        out_shape=jax.ShapeDtypeStruct(at_first.shape, at_first.dtype),
        in_specs=[SMEM, VMEM, VMEM],
        out_specs=VMEM,
        compiler_params=pltpu.CompilerParams(vmem_limit_bytes=SOME_ROOM),
        cost_estimate=pl.CostEstimate(
            flops=UNITS_FLOPS, bytes_accessed=1024 * 1024, transcendentals=0
        ),
    )(me.reshape(1), at_first, at_second)


def cache_whole(me, *pieces):
    def kernel(me_ref, *refs):
        sources, (whole_ref, sems) = refs[: len(GATHERED)], refs[len(GATHERED) :]
        here = me_ref[0]
        copies = []
        for n, (source, places) in enumerate(zip(sources, GATHERED)):
            for i, back in enumerate(places):
                if n == len(GATHERED) - 1:
                    back = back + (1 - 2 * i) * 4 * lax.rem(here, 2)
                for side in range(2):
                    owner = lax.rem(here + RING - back, RING)
                    micro = lax.rem(here // RING + side, 2)
                    head, half = owner // 2, lax.rem(owner, 2)
                    start = pl.multiple_of(half * (LENGTH // 2), LENGTH // 2)
                    for part in range(2):
                        column = pl.multiple_of(head * HEAD + part * KEY_WIDTH, HEAD)
                        copies.append(
                            pltpu.make_async_copy(
                                source.at[2 * i + side, :, pl.ds(part * HEAD, HEAD)],
                                whole_ref.at[micro, pl.ds(start, LENGTH // 2), pl.ds(column, HEAD)],
                                sems.at[len(copies)],
                            )
                        )
        for copy in copies:
            copy.start()
        for copy in copies:
            copy.wait()

    out = jax.ShapeDtypeStruct((MICROS, LENGTH, 2 * KEY_WIDTH), pieces[0].dtype)
    scratch = [pltpu.SemaphoreType.DMA((2 * SECTIONS,))]
    in_specs = [SMEM] + [VMEM] * len(pieces)
    return moving_call(kernel, out, scratch, in_specs)(me.reshape(1), *pieces)


def three_parts(rows):
    parts = []
    for i in range(GROUP):
        left = rows[i : i + 1]
        for _ in range(3):
            part = left.astype(jnp.bfloat16).astype(jnp.float32)
            parts.append(part)
            left = left - part
    parts.append(jnp.zeros_like(parts[0]))
    return jnp.concatenate(parts, axis=0).astype(jnp.bfloat16)


def from_parts(parts):
    parts = parts.astype(jnp.float32)
    return jnp.concatenate(
        [
            parts[3 * i : 3 * i + 1] + parts[3 * i + 1 : 3 * i + 2] + parts[3 * i + 2 : 3 * i + 3]
            for i in range(GROUP)
        ],
        axis=0,
    )


def pack(whole, late, gains=None):
    tall = STACK if gains is None else STACK + TAIL

    def kernel(*refs):
        whole_ref, (out_ref, held, stacked, in_sems, out_sems) = refs[-6], refs[-5:]
        arriving = [
            pltpu.make_async_copy(whole_ref.at[place], held.at[owner], in_sems.at[owner])
            for owner, place in home_places(late)
        ]
        for copy in arriving:
            copy.start()
        if gains is not None:
            rows = [refs[0][:, i * HEAD : (i + 1) * HEAD] for i in range(HEADS)]
            parts = [
                three_parts(jnp.concatenate(rows[k * GROUP : (k + 1) * GROUP], axis=0))
                for k in range(KV_HEADS)
            ]
        leaving = []
        for owner in range(SECTIONS):
            if gains is not None:
                stacked[owner, STACK:] = parts[owner % RING // 2]
            arriving[owner].wait()
            for h in range(GROUP):
                stacked[owner, h * BLOCK : (h + 1) * BLOCK] = held[owner, :, h * HEAD : (h + 1) * HEAD]
            copy = pltpu.make_async_copy(stacked.at[owner], out_ref.at[owner], out_sems.at[owner])
            copy.start()
            leaving.append(copy)
        for copy in leaving:
            copy.wait()

    out = jax.ShapeDtypeStruct((SECTIONS, tall, HEAD), whole.dtype)
    scratch = [
        pltpu.VMEM((SECTIONS, BLOCK, WIDE), whole.dtype),
        pltpu.VMEM(out.shape, whole.dtype),
        pltpu.SemaphoreType.DMA((SECTIONS,)),
        pltpu.SemaphoreType.DMA((SECTIONS,)),
    ]
    if gains is None:
        return moving_call(kernel, out, scratch, [IN_HBM])(whole)
    return moving_call(kernel, out, scratch, [VMEM, IN_HBM], room=ALL_ROOM)(gains, whole)


def unpack(came, late, whole=None):
    def kernel(came_ref, *rest):
        if whole is None:
            out_ref, (held, spread, in_sems, out_sems) = rest[0], rest[1:]
        else:
            _, out_ref, gain_ref, spread, out_sems = rest
            held = came_ref
        if whole is None:
            arriving = [
                pltpu.make_async_copy(came_ref.at[owner], held.at[owner], in_sems.at[owner])
                for owner in range(SECTIONS)
            ]
            for copy in arriving:
                copy.start()
        leaving = []
        for owner, place in home_places(late):
            if whole is None:
                arriving[owner].wait()
            for h in range(GROUP):
                spread[owner, :, h * HEAD : (h + 1) * HEAD] = held[owner, h * BLOCK : (h + 1) * BLOCK]
            copy = pltpu.make_async_copy(spread.at[owner], out_ref.at[place], out_sems.at[owner])
            copy.start()
            leaving.append(copy)
        if whole is not None:
            for head in range(KV_HEADS):
                total = jnp.zeros((GROUP, HEAD), jnp.float32)
                for owner in (2 * head, 2 * head + 1, RING + 2 * head, RING + 2 * head + 1):
                    total += from_parts(held[owner, STACK:])
                for h in range(GROUP):
                    first = head * WIDE + h * HEAD
                    gain_ref[:, first : first + HEAD] = total[h : h + 1]
        for copy in leaving:
            copy.wait()

    out = jax.ShapeDtypeStruct((MICROS, LENGTH, HEADS * HEAD), came.dtype)
    scratch = [
        pltpu.VMEM((SECTIONS, BLOCK, WIDE), came.dtype),
        pltpu.SemaphoreType.DMA((SECTIONS,)),
    ]
    if whole is None:
        first = [pltpu.VMEM(came.shape, came.dtype), scratch[0], scratch[1], scratch[1]]
        return moving_call(kernel, out, first, [IN_HBM])(came)
    outs = [out, jax.ShapeDtypeStruct((1, HEADS * HEAD), jnp.float32)]
    return moving_call(kernel, outs, scratch, [VMEM, IN_HBM], {1: 0})(came, whole)


def with_gains(grads, gain_part):
    def kernel(gain_ref, _, out_ref, tails, sems):
        copies = []
        for s in range(SECTIONS):
            tails[s] = three_parts(gain_ref[s])
            copy = pltpu.make_async_copy(tails.at[s], out_ref.at[s, pl.ds(STACK, TAIL)], sems.at[s])
            copy.start()
            copies.append(copy)
        for copy in copies:
            copy.wait()

    out = jax.ShapeDtypeStruct(grads.shape, grads.dtype)
    scratch = [
        pltpu.VMEM((SECTIONS, TAIL, HEAD), grads.dtype),
        pltpu.SemaphoreType.DMA((SECTIONS,)),
    ]
    return moving_call(kernel, out, scratch, [VMEM, IN_HBM], {1: 0})(gain_part, grads)


def per_row(gains):
    return jnp.concatenate(
        [jnp.broadcast_to(gains[h : h + 1], (BLOCK, HEAD)) for h in range(GROUP)], axis=0
    )


def per_head(rows):
    sums = [
        jnp.sum(rows[h * BLOCK : (h + 1) * BLOCK], axis=0, keepdims=True) for h in range(GROUP)
    ]
    return jnp.concatenate(sums + [jnp.zeros((8 - GROUP, HEAD), jnp.float32)], axis=0)


def run_layers(saved_ref, gain_of, kv_ref, bias_ref, top_ref, grads_ref, cache_ref, add_gain):
    seen = bias_ref.shape[0]
    contract_last = (((1,), (1,)), ((), ()))
    contract_first = (((0,), (0,)), ((), ()))

    def layer(step, incoming):
        s = SECTIONS - 1 - step
        keys, values = kv_ref[:seen, :HEAD], kv_ref[:seen, HEAD:]
        gain = per_row(gain_of(s))
        saved = saved_ref[s, :STACK].astype(jnp.float32)
        queries = (saved * gain).astype(jnp.bfloat16)
        scores = lax.dot_general(keys, queries, contract_last, preferred_element_type=jnp.float32)
        scores = scores * (SCALE * LOG2E) + bias_ref[...]
        exp_terms = jnp.exp2(scores - jnp.max(scores, axis=0, keepdims=True))
        probs = exp_terms * (1.0 / jnp.sum(exp_terms, axis=0, keepdims=True))
        dprob = lax.dot_general(values, incoming, contract_last, preferred_element_type=jnp.float32)
        delta = jnp.sum(probs * dprob, axis=0, keepdims=True)
        dscore = (probs * (dprob - delta)).astype(jnp.bfloat16)
        dquery = SCALE * lax.dot_general(
            dscore, keys, contract_first, preferred_element_type=jnp.float32
        )
        cache_ref[:seen, :HEAD] += SCALE * jnp.dot(dscore, queries, preferred_element_type=jnp.float32)
        cache_ref[:seen, HEAD:] += jnp.dot(
            probs.astype(jnp.bfloat16), incoming, preferred_element_type=jnp.float32
        )
        add_gain(s, per_head(dquery * saved))
        grads = (incoming.astype(jnp.float32) + gain * dquery).astype(jnp.bfloat16)
        grads_ref[s, :STACK] = grads
        return grads

    top = jnp.concatenate([top_ref[:, h * HEAD : (h + 1) * HEAD] for h in range(GROUP)], axis=0)
    lax.fori_loop(0, SECTIONS, layer, top, unroll=2)


def late_kernel(saved_ref, kv_ref, bias_ref, top_ref, grads_ref, cache_ref, gain_ref, part_ref):
    for s in range(SECTIONS):
        gain_ref[s, :GROUP] = from_parts(saved_ref[s, STACK:])
    cache_ref[...] = jnp.zeros_like(cache_ref)

    def add_gain(s, part):
        part_ref[s] = part

    run_layers(
        saved_ref, lambda s: gain_ref[s], kv_ref, bias_ref, top_ref, grads_ref, cache_ref, add_gain
    )


def early_kernel(saved_ref, kv_ref, bias_ref, top_ref, cache_before, gain_ref, part_before,
                 grads_ref, cache_ref, part_ref):
    cache_ref[...] = cache_before[...]

    def add_gain(s, part):
        part_ref[s] = part_before[s] + part

    run_layers(
        saved_ref, lambda s: gain_ref[s], kv_ref, bias_ref, top_ref, grads_ref, cache_ref, add_gain
    )


def chain(kernel, saved, kv_unit, bias, top, grads_tall, *before):
    seen, columns = bias.shape
    shapes = [
        ((SECTIONS, grads_tall, HEAD), jnp.bfloat16),
        ((LENGTH, 2 * HEAD), jnp.float32),
        ((SECTIONS, 8, HEAD), jnp.float32),
    ]
    if not before:
        shapes.append(shapes[-1])
    return pl.pallas_call(
        kernel,
        out_shape=[jax.ShapeDtypeStruct(*shape) for shape in shapes],
        in_specs=[VMEM] * (4 + len(before)),
        out_specs=[VMEM] * len(shapes),
        compiler_params=pltpu.CompilerParams(vmem_limit_bytes=24 * 1024 * 1024),
        cost_estimate=pl.CostEstimate(
            flops=SECTIONS * 10 * columns * seen * HEAD,
            bytes_accessed=6 * 1024 * 1024,
            transcendentals=SECTIONS * columns * seen,
        ),
    )(saved, kv_unit, bias, top, *before)


def bias_of(segments, block, keys_seen):
    rows = jnp.tile(lax.dynamic_slice(segments, (block * BLOCK,), (BLOCK,)), GROUP)
    query_pos = block * BLOCK + jnp.tile(jnp.arange(BLOCK), GROUP)
    key_pos = jnp.arange(keys_seen)
    allowed = (key_pos[:, None] <= query_pos[None, :]) & (
        segments[:keys_seen, None] == rows[None, :]
    )
    return jnp.where(allowed, 0.0, MASKED).astype(jnp.float32)


def on_device(saved_inputs, query_gains, cache_slots, segment_ids, output_grad):
    me = lax.axis_index("section")
    micro, head, half = me // RING, me % RING // 2, me % 2

    segments = lax.dynamic_index_in_dim(segment_ids, micro, 0, keepdims=False)
    late_block, early_block = 3 - half, half

    def top_of(block):
        start = (micro, block * BLOCK, head * WIDE)
        return lax.dynamic_slice(output_grad, start, (1, BLOCK, WIDE))[0]

    late_bias = bias_of(segments, late_block, LENGTH)
    early_bias = bias_of(segments, early_block, LENGTH // 2)
    late_top, early_top = top_of(late_block), top_of(early_block)

    raw = cache_slots[0]
    across = moved(raw[1], [(0, RING)])
    late_saved = exchange(pack(saved_inputs[0], True, query_gains))
    ready = after(saved_inputs[0], late_bias, early_bias, late_top, early_top)
    early_packed = pack(ready, False)
    four = own_units(me, raw, after(across, early_packed))
    came = [moved(four[k], [(0, z), (RING, RING + z)]) for k, z in ((2, 5), (1, 2), (3, 7))]
    at_first = jnp.where(me % RING == 0, four[0], came[0] + came[1] + came[2])
    at_first = after(at_first, early_packed)
    onward = ((0, 1), (2, 3), (5, 4), (7, 6))
    at_second = moved(at_first, [(x + i, x + j) for x in (0, RING) for i, j in onward])
    kv_unit = pick(me, at_first, at_second)
    early_saved = exchange(after(early_packed, late_saved, at_first))

    late_grads, cache_part, gains, gain_part = chain(
        late_kernel, late_saved, kv_unit, late_bias, late_top, STACK,
    )
    late_home = exchange(late_grads)
    early_grads, cache_part, gain_part = chain(
        early_kernel, early_saved, kv_unit, early_bias, early_top, STACK + TAIL,
        cache_part, gains, gain_part,
    )
    halves = cache_part.reshape(2, LENGTH // 2, 2 * HEAD)
    theirs = lax.dynamic_index_in_dim(halves, 1 - half, 0, keepdims=False)
    theirs = swapped(theirs.astype(jnp.bfloat16), 1)
    for bit in (1, 2, 4, 8):
        gain_part = gain_part + swapped(gain_part, bit, "dp")
    early_grads = with_gains(early_grads, gain_part)

    early_home = exchange(after(early_grads, late_home))
    mine = lax.dynamic_index_in_dim(halves, half, 0, keepdims=False) + theirs
    mine = after(mine.astype(jnp.bfloat16), early_grads)
    came = [swapped(mine, bit) for bit in (4, 12, 8)]
    whole = unpack(late_home, True)
    both = jnp.stack([mine, came[2], came[0], came[1]])
    both = after(both, whole, early_home)
    inward = [(i, i // RING * RING + (i + 2 - 4 * (i % 2)) % RING) for i in range(SECTIONS)]
    pieces = [both, turned(both, 1), turned(both, -1), moved(both, inward)]
    cache_grad = cache_whole(me, *pieces)
    layer_out, gain_sum = unpack(early_home, False, whole)
    return (layer_out[None], cache_grad, gain_sum)


def solution(mesh):
    return jax.shard_map(
        on_device,
        mesh=mesh,
        in_specs=(
            P("section", "dp", None, None),
            P("section", None),
            P("section", "dp", None, None),
            P("dp", None),
            P("dp", None, None),
        ),
        out_specs=(P("section", "dp", None, None), P("dp", None, None), P("section", None)),
        check_vma=False,
    )
```
